256 devices in a mesh: section: 16 (over x, z_lo, core), dp: 16 (over y, z_hi).
Axes of the slice: x: 4, y: 4, z: 8 (z_hi: 4, z_lo: 2; z = z_hi * 2 + z_lo), core: 2. Of those that a mesh axis runs over, the one named last changes fastest.
Arguments:
- sent_act: bfloat16 [16, 4096, 4096], P('section', 'dp'), may hold values from -120 to 120
- sent_grad: bfloat16 [16, 4096, 4096], P('section', 'dp'), may hold values from -120 to 120
- embedded: bfloat16 [4096, 4096], P('dp'), may hold values from -120 to 120
- loss_grad: bfloat16 [4096, 4096], P('dp'), may hold values from -120 to 120
- micro_weight: float32 [16, 4], replicated, may hold values from 0.25 to 4
- order: int32 [16, 4], replicated, may hold values from 0 to 3, each once within a row
- assignment: int32 [16, 64], P('section'), may hold values from 0 to 16, as said below
- old_inverse: float32 [16, 64, 128, 128], P('section', 'dp'), may hold values from -3 to 3
Outputs:
- new_inverse: float32 [16, 64, 128, 128], P('section', 'dp')
The draws below stay inside these ranges and needn't reach their ends.
Inputs may be any that keep to these rules, and one draw needn't show every extreme that they name: assignment[s, b] names the replica that refreshes block b of section s, or is 16 where the block keeps its old inverse; in each section no replica is named more than 8 times, one replica exactly 8 times, and some block keeps its old inverse. `order`: each row is a permutation.
All inputs are finite; a program needn't handle non-finite values.
Results may differ from the reference program's by a relative error of at most 0.0003.
Values may be sent and summed in bfloat16 or wider, within the bound.
A program may use at most 64 MiB of HBM per device.

```python
import math
import jax
import jax.numpy as jnp
from jax import lax

D = 4096
BLK = 128
MB = 4
MROWS = 64
CAP = 8
SECTIONS = 16
REPLICAS = 16
TOKENS = 4096
NBLK = 64


def scaled_field(key, shape, scale_low, scale_high):
    row_key, col_key, normal_key = jax.random.split(key, 3)
    row_shape = shape[:-1] + (1,)
    col_shape = shape[:-2] + (1, shape[-1])
    row_scale = jnp.exp(jax.random.uniform(row_key, row_shape, jnp.float32, math.log(scale_low), math.log(scale_high)))
    col_scale = jnp.exp(jax.random.uniform(col_key, col_shape, jnp.float32, math.log(scale_low), math.log(scale_high)))
    normal_part = jnp.clip(jax.random.normal(normal_key, shape, jnp.float32), -6.0, 6.0)
    base = normal_part
    return base * row_scale * col_scale


def draw_sent_act(key, part):
    key = jax.random.fold_in(key, 3)
    return scaled_field(key, (SECTIONS, TOKENS, D), 0.3, 3.0).astype(jnp.bfloat16)


def draw_sent_grad(key, part):
    key = jax.random.fold_in(key, 5)
    return scaled_field(key, (SECTIONS, TOKENS, D), 0.3, 3.0).astype(jnp.bfloat16)


def draw_embedded(key, part):
    key = jax.random.fold_in(key, 7)
    return scaled_field(key, (TOKENS, D), 0.3, 3.0).astype(jnp.bfloat16)


def draw_loss_grad(key, part):
    key = jax.random.fold_in(key, 9)
    return scaled_field(key, (TOKENS, D), 0.3, 3.0).astype(jnp.bfloat16)


def draw_assignment(key, part):
    key = jax.random.fold_in(key, 11)

    def one_section(section_key):
        block_key, heavy_key, pool_key = jax.random.split(section_key, 3)
        blocks = jax.random.permutation(block_key, NBLK)
        heavy = jax.random.randint(heavy_key, (), 0, REPLICAS, dtype=jnp.int32)
        others = jnp.arange((REPLICAS - 1) * CAP, dtype=jnp.int32) // CAP
        others = others + (others >= heavy).astype(jnp.int32)
        pool = jnp.concatenate([others, jnp.full((NBLK,), REPLICAS, jnp.int32)])
        pool = jax.random.permutation(pool_key, pool)
        values = jnp.concatenate([jnp.full((CAP,), 1, jnp.int32) * heavy, jnp.full((1,), REPLICAS, jnp.int32), pool[:NBLK - CAP - 1]])
        return jnp.zeros((NBLK,), jnp.int32).at[blocks].set(values)
    return jax.vmap(one_section)(jax.random.split(key, SECTIONS))


def levels(own_key, extent, pieces, smallest, high):
    def one(position, shards_of):
        heights = jax.random.uniform(jax.random.fold_in(jax.random.fold_in(own_key, 6), position), (shards_of,), jnp.float32, smallest / len(pieces), high / len(pieces))
        return jnp.repeat(jnp.exp(heights), extent[position] // shards_of).reshape((-1,) + (1,) * (len(extent) - position - 1))

    factor_of = one(*pieces[0])
    for cut in pieces[1:]:
        factor_of = factor_of * one(*cut)
    return factor_of


def scatter_about(own_key, dims, deviation, reach, shards=(), held_as=jnp.bfloat16):
    level = levels(own_key, dims, shards, -0.22, 0.18) if shards else 1.0
    entries = jax.random.normal(own_key, dims, jnp.float32) * deviation * level
    return jnp.minimum(jnp.maximum(entries, -reach), reach).astype(held_as)


def setup_inputs(seed: int = 0) -> dict:
    keys = jax.random.split(jax.random.key(seed), 9)
    sent_act = draw_sent_act(jax.random.fold_in(keys[8], 71), 0)
    sent_grad = draw_sent_grad(jax.random.fold_in(keys[8], 71), 0)
    embedded = draw_embedded(jax.random.fold_in(keys[8], 71), 0)
    loss_grad = draw_loss_grad(jax.random.fold_in(keys[8], 71), 0)
    micro_weight = jnp.clip(jnp.exp(jax.random.uniform(keys[4], (REPLICAS, MB), jnp.float32, math.log(0.25), math.log(4.0))), 0.25, 4.0)
    order = jax.vmap(lambda own: jax.random.permutation(own, MB))(jax.random.split(keys[5], SECTIONS)).reshape((SECTIONS, MB)).astype(jnp.int32)
    assignment = draw_assignment(jax.random.fold_in(keys[8], 71), 0)
    old_inverse = scatter_about(keys[7], (SECTIONS, NBLK, BLK, BLK), 0.5, 3.0, ((0, 16), (1, 16)), jnp.float32)
    return {"sent_act": sent_act, "sent_grad": sent_grad, "embedded": embedded, "loss_grad": loss_grad, "micro_weight": micro_weight, "order": order, "assignment": assignment, "old_inverse": old_inverse}


damping = 0.1

def invert_blocks(factor):
    identity = jnp.broadcast_to(jnp.eye(factor.shape[-1], dtype=jnp.float32), factor.shape)
    lower_part = jnp.linalg.cholesky(factor)
    half_solve = lax.linalg.triangular_solve(lower_part, identity, left_side=True, lower=True)
    return lax.linalg.triangular_solve(lower_part, half_solve, left_side=True, lower=True, transpose_a=True)

def weighted_grams(rows, slot_weight):
    blocked = rows.astype(jnp.float32).reshape(REPLICAS, MB, MROWS, D // BLK, BLK)
    per_slot = jnp.einsum('rktbi,rktbj->rkbij', blocked, blocked, precision=lax.Precision.HIGHEST)
    return jnp.einsum('rk,rkbij->bij', slot_weight, per_slot, precision=lax.Precision.HIGHEST)

def reference(sent_act, sent_grad, embedded, loss_grad, micro_weight, order, assignment, old_inverse):
    weight_total = MROWS * jnp.sum(micro_weight)
    identity = jnp.eye(BLK, dtype=jnp.float32)

    def one_section(section_at):
        earlier_section = jnp.maximum(section_at - 1, 0)
        later_section = jnp.minimum(section_at + 1, SECTIONS - 1)
        inputs = jnp.where(section_at == 0, embedded, lax.dynamic_index_in_dim(sent_act, earlier_section, 0, keepdims=False))
        gradients = jnp.where(section_at == SECTIONS - 1, loss_grad, lax.dynamic_index_in_dim(sent_grad, later_section, 0, keepdims=False))
        order_in = lax.dynamic_index_in_dim(order, earlier_section, 0, keepdims=False)
        order_out = lax.dynamic_index_in_dim(order, later_section, 0, keepdims=False)
        weight_in = jnp.take(micro_weight, order_in, axis=1)
        weight_out = jnp.take(micro_weight, order_out, axis=1)
        gram_blocks = jnp.concatenate([weighted_grams(inputs, weight_in), weighted_grams(gradients, weight_out)], axis=0)
        fresh_inverse = invert_blocks(gram_blocks / weight_total + damping * identity)
        assign_row = lax.dynamic_index_in_dim(assignment, section_at, 0, keepdims=False)
        previous = lax.dynamic_index_in_dim(old_inverse, section_at, 0, keepdims=False)
        return jnp.where((assign_row < REPLICAS)[:, None, None], fresh_inverse, previous)
    return lax.map(one_section, jnp.arange(SECTIONS, dtype=jnp.int32))
```

```python
import jax
import jax.numpy as jnp
from jax import lax
from jax.experimental import pallas as pl
from jax.experimental.pallas import tpu as pltpu
from jax.sharding import PartitionSpec as P

D = 4096
BLK = 128
MB = 4
MROWS = 64
ROWS = MB * MROWS
NBLK = 64
OWN = 4
SIDE = 4
SECTIONS = 16
REPLICAS = 16
PACKED = BLK + 8
PANEL = 8
MESH = pl.DeviceIdType.MESH

damping = 0.1


def flip1(v):
    return v + 1 - 2 * (v % 2)


def flip2(v):
    return (v + 2) % 4


def flip3(v):
    return 3 - v


def spread(v, half):
    if half == 0:
        return flip2(v), flip1(v), flip3(v), v
    return flip2(v), flip3(v), flip1(v), v


def final_target(s, y):
    low, last, inner = 1 - y // 2, s // (SECTIONS - 1), (s + SECTIONS - 1) // SECTIONS
    to_s = s + low * (1 - last) - (1 - low) * inner
    to_y = y + 2 * low * last - 2 * (1 - low) * (1 - inner)
    return to_s, to_y


def final_source(s, y):
    low, last, inner = 1 - y // 2, s // (SECTIONS - 1), (s + SECTIONS - 1) // SECTIONS
    from_s = s - low * inner + (1 - low) * (1 - last)
    from_y = y + 2 * low * (1 - inner) - 2 * (1 - low) * last
    return from_s, from_y


def reduce_kernel(
    sent_act, sent_grad, embedded, loss_grad, micro_weight, order, out,
    rows, acc, got_y1, got_y2, got_z1, got_f, in_sem,
    y1_send, y1_recv, y2_send, y2_recv, z1_send, z1_recv, f_send, f_recv,
):
    s = lax.axis_index("section")
    r = lax.axis_index("dp")
    y, z = r // SIDE, r % SIDE

    def fetch(src, part):
        return pltpu.make_async_copy(src, rows.at[:, pl.ds(part * D, D)], in_sem.at[part])

    @pl.when(s < SECTIONS - 1)
    def _():
        fetch(sent_act.at[0], 0).start()

    @pl.when(s == SECTIONS - 1)
    def _():
        fetch(loss_grad, 0).start()

    @pl.when(s > 0)
    def _():
        fetch(sent_grad.at[0], 1).start()

    @pl.when(s == 0)
    def _():
        fetch(embedded, 1).start()

    barrier = pltpu.get_barrier_semaphore()
    from_s, from_y = final_source(s, y)
    greet = [(s, flip1(y), z), (s, flip3(y), z), (s, y, flip1(z)), (s, y, flip3(z))]
    greet += [(from_s, from_y, z), (from_s, from_y, flip1(z)), (from_s, from_y, flip3(z))]
    for to_s, to_y, to_z in greet:
        pl.semaphore_signal(
            barrier, inc=1, device_id=(to_s, to_y * SIDE + to_z), device_id_type=MESH
        )

    weights = []
    for slot in range(MB):
        batch = order[s, slot]
        weight = jnp.float32(0.0)
        for m in range(MB):
            weight = weight + jnp.where(batch == m, micro_weight[r, m], 0.0)
        weights.append(weight)

    row_at = lax.broadcasted_iota(jnp.int32, (BLK, BLK), 0)
    col_at = lax.broadcasted_iota(jnp.int32, (BLK, BLK), 1)

    def gram(first_column):
        total = None
        for slot in range(MB):
            piece = rows[slot * MROWS:(slot + 1) * MROWS,
                         pl.ds(pl.multiple_of(first_column, BLK), BLK)]
            term = lax.dot_general(
                piece, piece, (((0,), (0,)), ((), ())), preferred_element_type=jnp.float32
            )
            term = weights[slot] * term
            total = term if total is None else total + term
        return total

    def compute(chunk, first_y_slot):
        for half in range(2):
            y_order, z_order = spread(y, half), spread(z, half)

            def body(i, carry):
                z_slot = i % 2
                y_at = jnp.where(i // 2 == 0, y_order[first_y_slot], y_order[first_y_slot + 1])
                z_at = jnp.where(z_slot == 0, z_order[2 * chunk], z_order[2 * chunk + 1])
                column = ((y_at * SIDE + z_at) * OWN + 2 * half) * BLK
                one, two = gram(column), gram(column + BLK)
                place = acc.at[half, chunk, first_y_slot + i // 2, z_slot]
                place[:BLK, :] = jnp.where(row_at >= col_at, one, two)
                diagonal = jnp.sum(
                    jnp.where(row_at == col_at, two, 0.0), axis=0, keepdims=True
                )
                place[BLK:, :] = jnp.broadcast_to(diagonal, (8, BLK))
                return carry

            lax.fori_loop(0, 4, body, 0)

    def remote(src, dst, send, recv, to):
        return pltpu.make_async_remote_copy(
            src_ref=src, dst_ref=dst, send_sem=send, recv_sem=recv,
            device_id=(to[0], to[1] * SIDE + to[2]), device_id_type=MESH,
        )

    y_first = [flip1(y), flip3(y)]
    y_second = [flip3(y), flip1(y)]
    z_first = [flip1(z), flip3(z)]
    z_second = [flip3(z), flip1(z)]
    to_s, to_y = final_target(s, y)

    step_y1 = [[remote(acc.at[h, c, pl.ds(0, 2)], got_y1.at[h, c], y1_send.at[h, c],
                       y1_recv.at[h, c], (s, y_first[h], z)) for c in range(2)] for h in range(2)]
    step_y2 = [[remote(acc.at[h, c, 2], got_y2.at[h, c], y2_send.at[h, c],
                       y2_recv.at[h, c], (s, y_second[h], z)) for c in range(2)] for h in range(2)]
    step_z1 = [remote(acc.at[h, 0, 3], got_z1.at[h], z1_send.at[h], z1_recv.at[h],
                      (s, y, z_first[h])) for h in range(2)]
    step_f = [[remote(acc.at[h, 1, 3, 0], got_f.at[h, 0], f_send.at[h, 0], f_recv.at[h, 0],
                      (to_s, to_y, z_second[h])),
               remote(acc.at[h, 1, 3, 1], got_f.at[h, 1], f_send.at[h, 1], f_recv.at[h, 1],
                      (to_s, to_y, z))] for h in range(2)]

    for part in range(2):
        fetch(sent_act.at[0], part).wait()
    compute(0, 0)
    pl.semaphore_wait(barrier, len(greet))
    for h in range(2):
        step_y1[h][0].start()
    compute(1, 0)
    for h in range(2):
        step_y1[h][1].start()
    compute(0, 2)
    compute(1, 2)

    for c in range(2):
        for h in range(2):
            step_y1[h][c].wait_recv()
            acc[h, c, 2] = acc[h, c, 2] + got_y1[h, c, 0]
            step_y2[h][c].start()
            acc[h, c, 3] = acc[h, c, 3] + got_y1[h, c, 1]
    for h in range(2):
        step_y2[h][0].wait_recv()
        acc[h, 0, 3] = acc[h, 0, 3] + got_y2[h, 0]
        step_z1[h].start()
    for h in range(2):
        step_y2[h][1].wait_recv()
        acc[h, 1, 3] = acc[h, 1, 3] + got_y2[h, 1]
    for h in range(2):
        step_z1[h].wait_recv()
        for i in range(2):
            acc[h, 1, 3, i] = acc[h, 1, 3, i] + got_z1[h, i]
            step_f[h][i].start()
    for h in range(2):
        for c in range(2):
            step_y1[h][c].wait_send()
            step_y2[h][c].wait_send()
        step_z1[h].wait_send()
    for h in range(2):
        for i in range(2):
            step_f[h][i].wait_recv()
        out[h] = got_f[h, 0] + got_f[h, 1]
    for h in range(2):
        for i in range(2):
            step_f[h][i].wait_send()


def reduce_blocks(sent_act, sent_grad, embedded, loss_grad, micro_weight, order):
    dma = pltpu.SemaphoreType.DMA
    block = (PACKED, BLK)
    hbm, smem = pl.BlockSpec(memory_space=pl.ANY), pl.BlockSpec(memory_space=pltpu.SMEM)
    return pl.pallas_call(
        reduce_kernel,
        out_shape=jax.ShapeDtypeStruct((2,) + block, jnp.float32),
        in_specs=[hbm] * 4 + [smem] * 2,
        out_specs=pl.BlockSpec(memory_space=pltpu.VMEM),
        scratch_shapes=[
            pltpu.VMEM((ROWS, 2 * D), jnp.bfloat16),
            pltpu.VMEM((2, 2, 4, 2) + block, jnp.float32),
            pltpu.VMEM((2, 2, 2, 2) + block, jnp.float32),
            pltpu.VMEM((2, 2, 2) + block, jnp.float32),
            pltpu.VMEM((2, 2) + block, jnp.float32),
            pltpu.VMEM((2, 2) + block, jnp.float32),
            dma((2,)),
            dma((2, 2)), dma((2, 2)), dma((2, 2)), dma((2, 2)),
            dma((2,)), dma((2,)), dma((2, 2)), dma((2, 2)),
        ],
        compiler_params=pltpu.CompilerParams(
            collective_id=0, has_side_effects=True, vmem_limit_bytes=32 * 1024 * 1024
        ),
        name="gram_reduce",
    )(sent_act, sent_grad, embedded, loss_grad, micro_weight, order)


def split3(x):
    high = x.astype(jnp.bfloat16)
    rest = x - high.astype(jnp.float32)
    middle = rest.astype(jnp.bfloat16)
    low = (rest - middle.astype(jnp.float32)).astype(jnp.bfloat16)
    return high, middle, low


def invert_kernel(micro_weight, assignment, packed, old, out, work):
    r = lax.axis_index("dp")
    row_at = lax.broadcasted_iota(jnp.int32, (BLK, BLK), 0)
    col_at = lax.broadcasted_iota(jnp.int32, (BLK, BLK), 1)
    weight_sum = jnp.sum(
        jnp.sum(micro_weight[...], axis=1, keepdims=True), axis=0, keepdims=True
    )
    scale = 1.0 / (MROWS * weight_sum)
    shift = jnp.where(row_at == col_at, jnp.float32(damping), 0.0)
    for half in range(2):
        square = packed[half, :BLK, :]
        flipped = square.T
        one = jnp.where(row_at >= col_at, square, flipped)
        two = jnp.where(row_at < col_at, square, flipped)
        two = jnp.where(row_at == col_at, packed[half, BLK:BLK + 1, :], two)
        work[2 * half] = one * scale + shift
        work[2 * half + 1] = two * scale + shift

    sub = lax.broadcasted_iota(jnp.int32, (PANEL, BLK), 0)
    lane = lax.broadcasted_iota(jnp.int32, (PANEL, BLK), 1)

    def spread_row(x, k):
        return jnp.broadcast_to(x[k:k + 1, :], (PANEL, BLK))

    for p in range(BLK // PANEL):
        start = p * PANEL
        inside = (lane >= start) & (lane < start + PANEL)
        panel_cols = (col_at >= start) & (col_at < start + PANEL)
        original = [work[m, start:start + PANEL, :] for m in range(OWN)]
        state = list(original)
        columns = [
            [jnp.broadcast_to(x[:, start + j:start + j + 1], (PANEL, BLK)) for j in range(PANEL)]
            for x in original
        ]
        for k in range(PANEL):
            for m in range(OWN):
                here = columns[m][k]
                inverse = 1.0 / spread_row(here, k)
                marked = jnp.where(lane == start + k, jnp.where(sub == k, 1.0, 0.0), state[m])
                pivot_row = spread_row(marked, k) * inverse
                state[m] = jnp.where(sub == k, pivot_row, marked - here * pivot_row)
                for j in range(k + 1, PANEL):
                    step = spread_row(columns[m][j], k) * inverse
                    columns[m][j] = jnp.where(sub == k, step, columns[m][j] - here * step)
        for m in range(OWN):
            swept = jnp.where(inside, -state[m], state[m])
            h0, m0, l0 = split3(original[m])
            h1, m1, l1 = split3(swept)
            left = jnp.concatenate([h0, h0, m0, m0, h0, l0], axis=0)
            right = jnp.concatenate([h1, m1, h1, m1, l1, h1], axis=0)
            update = lax.dot_general(
                left, right, (((0,), (0,)), ((), ())), preferred_element_type=jnp.float32
            )
            work[m] = jnp.where(panel_cols, 0.0, work[m]) - update
            work[m, start:start + PANEL, :] = swept

    for m in range(OWN):
        refreshed = assignment[0, r * OWN + m] < REPLICAS
        out[0, m] = jnp.where(refreshed, -work[m], old[0, m])


def invert_blocks(micro_weight, assignment, packed, old_inverse):
    vmem, smem = pl.BlockSpec(memory_space=pltpu.VMEM), pl.BlockSpec(memory_space=pltpu.SMEM)
    return pl.pallas_call(
        invert_kernel,
        out_shape=jax.ShapeDtypeStruct(old_inverse.shape, jnp.float32),
        in_specs=[vmem, smem, vmem, vmem],
        out_specs=vmem,
        scratch_shapes=[pltpu.VMEM((OWN, BLK, BLK), jnp.float32)],
        compiler_params=pltpu.CompilerParams(vmem_limit_bytes=32 * 1024 * 1024),
        name="invert",
    )(micro_weight, assignment, packed, old_inverse)


def shards(sent_act, sent_grad, embedded, loss_grad, micro_weight, order, assignment, old_inverse):
    packed = reduce_blocks(sent_act, sent_grad, embedded, loss_grad, micro_weight, order)
    return invert_blocks(micro_weight, assignment, packed, old_inverse)


def solution(mesh):
    in_specs = (
        P("section", "dp", None),
        P("section", "dp", None),
        P("dp", None),
        P("dp", None),
        P(),
        P(),
        P("section", None),
        P("section", "dp", None, None),
    )
    out_specs = P("section", "dp", None, None)
    return jax.shard_map(shards, mesh=mesh, in_specs=in_specs, out_specs=out_specs, check_vma=False)
```

```python
import jax
import jax.numpy as jnp
from jax import lax
from jax.experimental import pallas as pl
from jax.experimental.pallas import tpu as pltpu
from jax.sharding import PartitionSpec as P

D = 4096
BLK = 128
MB = 4
MROWS = 64
ROWS = MB * MROWS
NBLK = 64
OWN = 4
SIDE = 4
SECTIONS = 16
REPLICAS = 16
PACKED = BLK + 8
PANEL = 8
VMEM_LIMIT = 60 * 1024 * 1024
MESH = pl.DeviceIdType.MESH

damping = 0.1


def flip1(v):
    return v + 1 - 2 * (v % 2)


def flip2(v):
    return (v + 2) % 4


def flip3(v):
    return 3 - v


def spread(v, half):
    if half == 0:
        return flip2(v), flip1(v), flip3(v), v
    return flip2(v), flip3(v), flip1(v), v


def final_target(s, y):
    low, last, inner = 1 - y // 2, s // (SECTIONS - 1), (s + SECTIONS - 1) // SECTIONS
    to_s = s + low * (1 - last) - (1 - low) * inner
    to_y = y + 2 * low * last - 2 * (1 - low) * (1 - inner)
    return to_s, to_y


def final_source(s, y):
    low, last, inner = 1 - y // 2, s // (SECTIONS - 1), (s + SECTIONS - 1) // SECTIONS
    from_s = s - low * inner + (1 - low) * (1 - last)
    from_y = y + 2 * low * (1 - inner) - 2 * (1 - low) * last
    return from_s, from_y


def reduce_kernel(
    sent_act, sent_grad, embedded, loss_grad, micro_weight, order, out,
    rows, give, keep, got_y1, got_y2, got_z1, got_f, in_sem,
    y1_send, y1_recv, y2_send, y2_recv, z1_send, z1_recv, f_send, f_recv,
):
    s = lax.axis_index("section")
    r = lax.axis_index("dp")
    y, z = r // SIDE, r % SIDE
    fetch_order = (flip2(z), flip1(z), flip3(z), z)

    def fetch(src, to_y, place):
        column = (to_y * SIDE + fetch_order[place]) * OWN * BLK
        wide = pl.ds(pl.multiple_of(column, OWN * BLK), OWN * BLK)
        narrow = pl.ds(pl.multiple_of(column - to_y // 2 * D, OWN * BLK), OWN * BLK)
        return pltpu.make_async_copy(
            src.at[:, narrow], rows.at[:, wide], in_sem.at[place, to_y]
        )

    for place in range(SIDE):
        @pl.when(s < SECTIONS - 1)
        def _():
            for to_y in range(2):
                fetch(sent_act.at[0], to_y, place).start()

        @pl.when(s == SECTIONS - 1)
        def _():
            for to_y in range(2):
                fetch(loss_grad, to_y, place).start()

        @pl.when(s > 0)
        def _():
            for to_y in range(2, 4):
                fetch(sent_grad.at[0], to_y, place).start()

        @pl.when(s == 0)
        def _():
            for to_y in range(2, 4):
                fetch(embedded, to_y, place).start()

    def fetched(place):
        for to_y in range(SIDE):
            fetch(sent_act.at[0], to_y, place).wait()

    barrier = pltpu.get_barrier_semaphore()
    from_s, from_y = final_source(s, y)
    greet = [(s, flip1(y), z), (s, flip3(y), z), (s, y, flip1(z)), (s, y, flip3(z))]
    greet += [(from_s, from_y, z), (from_s, from_y, flip1(z)), (from_s, from_y, flip3(z))]
    for to_s, to_y, to_z in greet:
        pl.semaphore_signal(
            barrier, inc=1, device_id=(to_s, to_y * SIDE + to_z), device_id_type=MESH
        )

    weights = []
    for slot in range(MB):
        batch = order[slot, s]
        weight = jnp.float32(0.0)
        for m in range(MB):
            weight = weight + jnp.where(batch == m, micro_weight[m, r], 0.0)
        weights.append(weight)

    row_at = lax.broadcasted_iota(jnp.int32, (BLK, BLK), 0)
    col_at = lax.broadcasted_iota(jnp.int32, (BLK, BLK), 1)
    blank = jnp.zeros((MROWS, BLK), jnp.bfloat16)
    y_orders, z_orders = [spread(y, h) for h in range(2)], [spread(z, h) for h in range(2)]

    def unit(half, y_at, z_at):
        column = ((y_at * SIDE + z_at) * OWN + 2 * half) * BLK
        total = None
        for slot in range(MB):
            at = pl.ds(slot * MROWS, MROWS)
            one = rows[at, pl.ds(pl.multiple_of(column, 2 * BLK), BLK)]
            two = rows[at, pl.ds(pl.multiple_of(column + BLK, BLK), BLK)]
            left = jnp.concatenate([one, two], axis=0)
            right = jnp.concatenate(
                [jnp.concatenate([one, blank], axis=1), jnp.concatenate([blank, two], axis=1)],
                axis=0,
            )
            term = weights[slot] * lax.dot_general(
                left, right, (((0,), (0,)), ((), ())), preferred_element_type=jnp.float32
            )
            total = term if total is None else total + term
        first, second = total[:, :BLK], total[:, BLK:]
        square = jnp.where(row_at >= col_at, first, second)
        diagonal = jnp.sum(jnp.where(row_at == col_at, second, 0.0), axis=0, keepdims=True)
        return square, diagonal

    def compute_give(chunk):
        for half in range(2):
            for i in range(2):
                square, diagonal = unit(half, y_orders[half][i], z_orders[half][chunk])
                give[half, chunk, i * BLK:(i + 1) * BLK, :] = square
                if i == 0:
                    give[half, chunk, 2 * BLK:, :] = jnp.broadcast_to(diagonal, (8, BLK))
                else:
                    give[half, chunk, 2 * BLK + 1:2 * BLK + 2, :] = diagonal

    def compute_keep(chunk):
        for half in range(2):
            for i in range(2):
                square, diagonal = unit(half, y_orders[half][2 + i], z_orders[half][chunk])
                keep[half, chunk, i, :BLK, :] = square
                keep[half, chunk, i, BLK:, :] = jnp.broadcast_to(diagonal, (8, BLK))

    def remote(src, dst, send, recv, to):
        return pltpu.make_async_remote_copy(
            src_ref=src, dst_ref=dst, send_sem=send, recv_sem=recv,
            device_id=(to[0], to[1] * SIDE + to[2]), device_id_type=MESH,
        )

    y_first = [flip1(y), flip3(y)]
    y_second = [flip3(y), flip1(y)]
    z_first = [flip1(z), flip3(z)]
    z_second = [flip3(z), flip1(z)]
    to_s, to_y = final_target(s, y)
    halves, chunks = range(2), range(SIDE)

    step_y1 = [[remote(give.at[h, c], got_y1.at[h, c], y1_send.at[h, c], y1_recv.at[h, c],
                       (s, y_first[h], z)) for c in chunks] for h in halves]
    step_y2 = [[remote(keep.at[h, c, 0], got_y2.at[h, c], y2_send.at[h, c], y2_recv.at[h, c],
                       (s, y_second[h], z)) for c in chunks] for h in halves]
    step_z1 = [remote(keep.at[h, 0, 1], got_z1.at[h], z1_send.at[h], z1_recv.at[h],
                      (s, y, z_first[h])) for h in halves]
    step_f = [[remote(keep.at[h, 1 + j, 1], got_f.at[h, j], f_send.at[h, j], f_recv.at[h, j],
                      (to_s, to_y, to_z))
               for j, to_z in enumerate((z_first[h], z_second[h], z))] for h in halves]

    def add_first(h, c, i):
        keep[h, c, i, :BLK] = keep[h, c, i, :BLK] + got_y1[h, c, i * BLK:(i + 1) * BLK]
        at = 2 * BLK + i
        keep[h, c, i, BLK:BLK + 1] = keep[h, c, i, BLK:BLK + 1] + got_y1[h, c, at:at + 1]

    def finish(c):
        for h in halves:
            step_y2[h][c].wait_recv()
            if c == 2:
                step_z1[h].wait_recv()
                keep[h, c, 1] = keep[h, c, 1] + (got_y2[h, c] + got_z1[h])
            else:
                keep[h, c, 1] = keep[h, c, 1] + got_y2[h, c]
            (step_z1[h] if c == 0 else step_f[h][c - 1]).start()

    fetched(0)
    compute_give(0)
    pl.semaphore_wait(barrier, len(greet))
    for h in halves:
        step_y1[h][0].start()
    fetched(1)
    fetched(2)
    compute_give(1)
    for h in halves:
        step_y1[h][1].start()
    compute_give(2)
    fetched(3)
    for c in chunks:
        if c == 1:
            compute_give(3)
        compute_keep(c)
        for h in halves:
            step_y1[h][c].wait_recv()
            add_first(h, c, 0)
            step_y2[h][c].start()
            if c + 2 < SIDE:
                step_y1[h][c + 2].start()
            add_first(h, c, 1)
        if c > 0:
            finish(c - 1)
    finish(SIDE - 1)
    for h in halves:
        for c in chunks:
            step_y1[h][c].wait_send()
            step_y2[h][c].wait_send()
        step_z1[h].wait_send()
    for h in halves:
        for j in range(3):
            step_f[h][j].wait_recv()
        out[h] = got_f[h, 0] + got_f[h, 1] + got_f[h, 2]
    for h in halves:
        for j in range(3):
            step_f[h][j].wait_send()


def reduce_blocks(sent_act, sent_grad, embedded, loss_grad, micro_weight, order):
    dma = pltpu.SemaphoreType.DMA
    block = (PACKED, BLK)
    pair = (2 * BLK + 8, BLK)
    hbm, smem = pl.BlockSpec(memory_space=pltpu.HBM), pl.BlockSpec(memory_space=pltpu.SMEM)
    return pl.pallas_call(
        reduce_kernel,
        out_shape=jax.ShapeDtypeStruct((2,) + block, jnp.float32),
        in_specs=[hbm] * 4 + [smem] * 2,
        out_specs=pl.BlockSpec(memory_space=pltpu.VMEM),
        scratch_shapes=[
            pltpu.VMEM((ROWS, 2 * D), jnp.bfloat16),
            pltpu.VMEM((2, SIDE) + pair, jnp.float32),
            pltpu.VMEM((2, SIDE, 2) + block, jnp.float32),
            pltpu.VMEM((2, SIDE) + pair, jnp.float32),
            pltpu.VMEM((2, SIDE) + block, jnp.float32),
            pltpu.VMEM((2,) + block, jnp.float32),
            pltpu.VMEM((2, 3) + block, jnp.float32),
            dma((SIDE, SIDE)),
            dma((2, SIDE)), dma((2, SIDE)), dma((2, SIDE)), dma((2, SIDE)),
            dma((2,)), dma((2,)), dma((2, 3)), dma((2, 3)),
        ],
        compiler_params=pltpu.CompilerParams(
            collective_id=0, has_side_effects=True, vmem_limit_bytes=VMEM_LIMIT
        ),
        name="gram_reduce",
    )(sent_act, sent_grad, embedded, loss_grad, micro_weight, order)


def split3(x):
    high = x.astype(jnp.bfloat16)
    rest = x - high.astype(jnp.float32)
    middle = rest.astype(jnp.bfloat16)
    low = (rest - middle.astype(jnp.float32)).astype(jnp.bfloat16)
    return high, middle, low


def invert_kernel(micro_weight, assignment, packed, old, out, work):
    r = lax.axis_index("dp")
    row_at = lax.broadcasted_iota(jnp.int32, (BLK, BLK), 0)
    col_at = lax.broadcasted_iota(jnp.int32, (BLK, BLK), 1)
    weight_sum = jnp.sum(
        jnp.sum(micro_weight[...], axis=1, keepdims=True), axis=0, keepdims=True
    )
    scale = 1.0 / (MROWS * weight_sum)
    shift = jnp.where(row_at == col_at, jnp.float32(damping), 0.0)
    for half in range(2):
        square = packed[half, :BLK, :]
        flipped = square.T
        one = jnp.where(row_at >= col_at, square, flipped)
        two = jnp.where(row_at < col_at, square, flipped)
        two = jnp.where(row_at == col_at, packed[half, BLK:BLK + 1, :], two)
        work[2 * half] = one * scale + shift
        work[2 * half + 1] = two * scale + shift

    sub = lax.broadcasted_iota(jnp.int32, (PANEL, BLK), 0)
    lane = lax.broadcasted_iota(jnp.int32, (PANEL, BLK), 1)

    def spread_row(x, k):
        return jnp.broadcast_to(x[k:k + 1, :], (PANEL, BLK))

    for p in range(BLK // PANEL):
        start = p * PANEL
        inside = (lane >= start) & (lane < start + PANEL)
        panel_cols = (col_at >= start) & (col_at < start + PANEL)
        original = [work[m, start:start + PANEL, :] for m in range(OWN)]
        state = list(original)
        columns = [
            [jnp.broadcast_to(x[:, start + j:start + j + 1], (PANEL, BLK)) for j in range(PANEL)]
            for x in original
        ]
        for k in range(PANEL):
            for m in range(OWN):
                here = columns[m][k]
                inverse = 1.0 / spread_row(here, k)
                marked = jnp.where(lane == start + k, jnp.where(sub == k, 1.0, 0.0), state[m])
                pivot_row = spread_row(marked, k) * inverse
                state[m] = jnp.where(sub == k, pivot_row, marked - here * pivot_row)
                for j in range(k + 1, PANEL):
                    step = spread_row(columns[m][j], k) * inverse
                    columns[m][j] = jnp.where(sub == k, step, columns[m][j] - here * step)
        for m in range(OWN):
            swept = jnp.where(inside, -state[m], state[m])
            h0, m0, l0 = split3(original[m])
            h1, m1, l1 = split3(swept)
            left = jnp.concatenate([h0, h0, m0, m0, h0, l0], axis=0)
            right = jnp.concatenate([h1, m1, h1, m1, l1, h1], axis=0)
            update = lax.dot_general(
                left, right, (((0,), (0,)), ((), ())), preferred_element_type=jnp.float32
            )
            work[m] = jnp.where(panel_cols, 0.0, work[m]) - update
            work[m, start:start + PANEL, :] = swept

    for m in range(OWN):
        refreshed = assignment[0, r * OWN + m] < REPLICAS
        out[0, m] = jnp.where(refreshed, -work[m], old[0, m])


def invert_blocks(micro_weight, assignment, packed, old_inverse):
    vmem, smem = pl.BlockSpec(memory_space=pltpu.VMEM), pl.BlockSpec(memory_space=pltpu.SMEM)
    return pl.pallas_call(
        invert_kernel,
        out_shape=jax.ShapeDtypeStruct(old_inverse.shape, jnp.float32),
        in_specs=[vmem, smem, vmem, vmem],
        out_specs=vmem,
        scratch_shapes=[pltpu.VMEM((OWN, BLK, BLK), jnp.float32)],
        compiler_params=pltpu.CompilerParams(vmem_limit_bytes=VMEM_LIMIT),
        name="invert",
    )(micro_weight, assignment, packed, old_inverse)


def shards(sent_act, sent_grad, embedded, loss_grad, micro_weight, order, assignment, old_inverse):
    micro_weight = micro_weight.T
    packed = reduce_blocks(sent_act, sent_grad, embedded, loss_grad, micro_weight, order.T)
    return invert_blocks(micro_weight, assignment, packed, old_inverse)


def solution(mesh):
    in_specs = (
        P("section", "dp", None),
        P("section", "dp", None),
        P("dp", None),
        P("dp", None),
        P(),
        P(),
        P("section", None),
        P("section", "dp", None, None),
    )
    out_specs = P("section", "dp", None, None)
    return jax.shard_map(shards, mesh=mesh, in_specs=in_specs, out_specs=out_specs, check_vma=False)
```

```python
import jax
import jax.numpy as jnp
from jax import lax
from jax.experimental import pallas as pl
from jax.experimental.pallas import tpu as pltpu
from jax.sharding import PartitionSpec as P

D = 4096
BLK = 128
MB = 4
MROWS = 64
ROWS = MB * MROWS
NBLK = 64
OWN = 4
SIDE = 4
SECTIONS = 16
REPLICAS = 16
PACKED = BLK + 8
TOP = 88
LOW = BLK - TOP
PANEL = 8
ROUNDS = 2
LIMIT = 1e-6
VMEM_LIMIT = 60 * 1024 * 1024
MESH = pl.DeviceIdType.MESH

damping = 0.1


def flip1(v):
    return v + 1 - 2 * (v % 2)


def flip2(v):
    return (v + 2) % 4


def flip3(v):
    return 3 - v


def spread(v, half):
    if half == 0:
        return flip2(v), flip1(v), flip3(v), v
    return flip2(v), flip3(v), flip1(v), v


def final_target(s, y):
    low, last, inner = 1 - y // 2, s // (SECTIONS - 1), (s + SECTIONS - 1) // SECTIONS
    to_s = s + low * (1 - last) - (1 - low) * inner
    to_y = y + 2 * low * last - 2 * (1 - low) * (1 - inner)
    return to_s, to_y


def final_source(s, y):
    low, last, inner = 1 - y // 2, s // (SECTIONS - 1), (s + SECTIONS - 1) // SECTIONS
    from_s = s - low * inner + (1 - low) * (1 - last)
    from_y = y + 2 * low * (1 - inner) - 2 * (1 - low) * last
    return from_s, from_y


def reduce_kernel(
    sent_act, sent_grad, embedded, loss_grad, micro_weight, order, out,
    rows, give, keep, got_y1, got_y2, got_z1, got_f,
    low_give, low_keep, low_z1, low_y1, low_y2, low_f, in_sem,
    y1_send, y1_recv, y2_send, y2_recv, z1_send, z1_recv, f_send, f_recv,
    lz1_send, lz1_recv, ly1_send, ly1_recv, ly2_send, ly2_recv, lf_send, lf_recv,
):
    s = lax.axis_index("section")
    r = lax.axis_index("dp")
    y, z = r // SIDE, r % SIDE

    barrier = pltpu.get_barrier_semaphore()
    from_s, from_y = final_source(s, y)
    greet = [(s, flip1(y), z), (s, flip3(y), z), (s, y, flip1(z)), (s, y, flip3(z))]
    greet += [(from_s, from_y, z), (from_s, from_y, flip1(z)), (from_s, from_y, flip3(z))]
    for to_s, to_y, to_z in greet:
        pl.semaphore_signal(
            barrier, inc=1, device_id=(to_s, to_y * SIDE + to_z), device_id_type=MESH
        )

    fetch_order = (flip2(z), flip1(z), flip3(z), z)

    def fetch(src, to_y, place):
        column = (to_y * SIDE + fetch_order[place]) * OWN * BLK
        wide = pl.ds(pl.multiple_of(column, OWN * BLK), OWN * BLK)
        narrow = pl.ds(pl.multiple_of(column - to_y // 2 * D, OWN * BLK), OWN * BLK)
        return pltpu.make_async_copy(
            src.at[:, narrow], rows.at[:, wide], in_sem.at[place, to_y]
        )

    for place in range(SIDE):
        @pl.when(s < SECTIONS - 1)
        def _():
            for to_y in range(2):
                fetch(sent_act.at[0], to_y, place).start()

        @pl.when(s == SECTIONS - 1)
        def _():
            for to_y in range(2):
                fetch(loss_grad, to_y, place).start()

        @pl.when(s > 0)
        def _():
            for to_y in range(2, 4):
                fetch(sent_grad.at[0], to_y, place).start()

        @pl.when(s == 0)
        def _():
            for to_y in range(2, 4):
                fetch(embedded, to_y, place).start()

    def fetched(place):
        for to_y in range(SIDE):
            fetch(sent_act.at[0], to_y, place).wait()

    weights = []
    for slot in range(MB):
        batch = order[slot, s]
        weight = jnp.float32(0.0)
        for m in range(MB):
            weight = weight + jnp.where(batch == m, micro_weight[m, r], 0.0)
        weights.append(weight)

    row_at = lax.broadcasted_iota(jnp.int32, (BLK, BLK), 0)
    col_at = lax.broadcasted_iota(jnp.int32, (BLK, BLK), 1)
    blank = jnp.zeros((MROWS, BLK), jnp.bfloat16)
    y_orders, z_orders = [spread(y, h) for h in range(2)], [spread(z, h) for h in range(2)]

    def unit(half, y_at, z_at):
        column = ((y_at * SIDE + z_at) * OWN + 2 * half) * BLK
        total = None
        for slot in range(MB):
            at = pl.ds(slot * MROWS, MROWS)
            one = rows[at, pl.ds(pl.multiple_of(column, 2 * BLK), BLK)]
            two = rows[at, pl.ds(pl.multiple_of(column + BLK, BLK), BLK)]
            left = jnp.concatenate([one, two], axis=0)
            right = jnp.concatenate(
                [jnp.concatenate([one, blank], axis=1), jnp.concatenate([blank, two], axis=1)],
                axis=0,
            )
            term = weights[slot] * lax.dot_general(
                left, right, (((0,), (0,)), ((), ())), preferred_element_type=jnp.float32
            )
            total = term if total is None else total + term
        first, second = total[:, :BLK], total[:, BLK:]
        square = jnp.where(row_at >= col_at, first, second)
        diagonal = jnp.sum(jnp.where(row_at == col_at, second, 0.0), axis=0, keepdims=True)
        return square, diagonal

    def compute(chunk):
        for half in range(2):
            for i in range(SIDE):
                square, diagonal = unit(half, y_orders[half][i], z_orders[half][chunk])
                top, bottom = square[:TOP], square[TOP:]
                if i < 2:
                    give[half, chunk, i * TOP:(i + 1) * TOP, :] = top
                    if i == 0:
                        give[half, chunk, 2 * TOP:, :] = jnp.broadcast_to(diagonal, (8, BLK))
                    else:
                        give[half, chunk, 2 * TOP + 1:2 * TOP + 2, :] = diagonal
                else:
                    keep[half, chunk, i - 2, :TOP, :] = top
                    keep[half, chunk, i - 2, TOP:, :] = jnp.broadcast_to(diagonal, (8, BLK))
                (low_give if chunk < 2 else low_keep)[half, i, chunk % 2] = bottom

    def remote(src, dst, send, recv, to):
        return pltpu.make_async_remote_copy(
            src_ref=src, dst_ref=dst, send_sem=send, recv_sem=recv,
            device_id=(to[0], to[1] * SIDE + to[2]), device_id_type=MESH,
        )

    y_first = [flip1(y), flip3(y)]
    y_second = [flip3(y), flip1(y)]
    z_first = [flip1(z), flip3(z)]
    z_second = [flip3(z), flip1(z)]
    to_s, to_y = final_target(s, y)
    halves, chunks = range(2), range(SIDE)

    step_y1 = [[remote(give.at[h, c], got_y1.at[h, c], y1_send.at[h, c], y1_recv.at[h, c],
                       (s, y_first[h], z)) for c in chunks] for h in halves]
    step_y2 = [[remote(keep.at[h, c, 0], got_y2.at[h, c], y2_send.at[h, c], y2_recv.at[h, c],
                       (s, y_second[h], z)) for c in chunks] for h in halves]
    step_z1 = [remote(keep.at[h, 0, 1], got_z1.at[h], z1_send.at[h], z1_recv.at[h],
                      (s, y, z_first[h])) for h in halves]
    step_f = [[remote(keep.at[h, 1 + j, 1], got_f.at[h, j], f_send.at[h, j], f_recv.at[h, j],
                      (to_s, to_y, to_z))
               for j, to_z in enumerate((z_first[h], z_second[h], z))] for h in halves]
    low_step_z1 = [[remote(low_give.at[h, i], low_z1.at[h, i], lz1_send.at[h, i],
                           lz1_recv.at[h, i], (s, y, z_first[h])) for i in chunks] for h in halves]
    low_step_y1 = [[remote(low_keep.at[h, i], low_y1.at[h, i], ly1_send.at[h, i],
                           ly1_recv.at[h, i], (s, y_first[h], z)) for i in range(2)] for h in halves]
    low_step_y2 = [remote(low_keep.at[h, 2], low_y2.at[h], ly2_send.at[h], ly2_recv.at[h],
                          (s, y_second[h], z)) for h in halves]
    low_step_f = [[remote(low_keep.at[h, 3, j], low_f.at[h, j], lf_send.at[h, j],
                          lf_recv.at[h, j], (to_s, to_y, to_z))
                   for j, to_z in enumerate((z_second[h], z))] for h in halves]

    def add_first(h, c, i):
        keep[h, c, i, :TOP] = keep[h, c, i, :TOP] + got_y1[h, c, i * TOP:(i + 1) * TOP]
        at = 2 * TOP + i
        keep[h, c, i, TOP:TOP + 1] = keep[h, c, i, TOP:TOP + 1] + got_y1[h, c, at:at + 1]

    def after_y1(c):
        for h in halves:
            step_y1[h][c].wait_recv()
            add_first(h, c, 0)
            step_y2[h][c].start()
            if c + 2 < SIDE:
                step_y1[h][c + 2].start()
            add_first(h, c, 1)

    def after_y2(c):
        for h in halves:
            step_y2[h][c].wait_recv()
            if c == 2:
                step_z1[h].wait_recv()
                keep[h, c, 1] = keep[h, c, 1] + (got_y2[h, c] + got_z1[h])
            else:
                keep[h, c, 1] = keep[h, c, 1] + got_y2[h, c]
            (step_z1[h] if c == 0 else step_f[h][c - 1]).start()

    def after_low_z1(i):
        for h in halves:
            low_step_z1[h][i].wait_recv()
            low_keep[h, i] = low_keep[h, i] + low_z1[h, i]
            if i < 2:
                low_step_y1[h][i].start()

    def after_low_y1():
        for h in halves:
            for i in range(2):
                low_step_y1[h][i].wait_recv()
                low_keep[h, 2 + i] = low_keep[h, 2 + i] + low_y1[h, i]
                if i == 0:
                    low_step_y2[h].start()

    def after_low_y2():
        for h in halves:
            low_step_y2[h].wait_recv()
            low_keep[h, 3] = low_keep[h, 3] + low_y2[h]
            for j in range(2):
                low_step_f[h][j].start()

    fetched(0)
    compute(0)
    pl.semaphore_wait(barrier, len(greet))
    for h in halves:
        step_y1[h][0].start()
    fetched(1)
    fetched(2)
    compute(1)
    for h in halves:
        step_y1[h][1].start()
        for i in chunks:
            low_step_z1[h][i].start()
    compute(2)
    fetched(3)
    compute(3)
    after_y1(0)
    after_low_z1(0)
    after_low_z1(1)
    after_y1(1)
    after_y2(0)
    after_low_z1(2)
    after_low_z1(3)
    after_y1(2)
    after_low_y1()
    after_y2(1)
    after_y1(3)
    after_low_y2()
    after_y2(2)
    after_y2(3)
    for h in halves:
        for c in chunks:
            step_y1[h][c].wait_send()
            step_y2[h][c].wait_send()
            low_step_z1[h][c].wait_send()
        step_z1[h].wait_send()
        low_step_y1[h][0].wait_send()
        low_step_y1[h][1].wait_send()
        low_step_y2[h].wait_send()
    for h in halves:
        for j in range(2):
            low_step_f[h][j].wait_recv()
        out[h, TOP:BLK] = low_f[h, 0] + low_f[h, 1]
    for h in halves:
        for j in range(3):
            step_f[h][j].wait_recv()
        total = got_f[h, 0] + got_f[h, 1] + got_f[h, 2]
        out[h, :TOP] = total[:TOP]
        out[h, BLK:] = total[TOP:]
    for h in halves:
        for j in range(3):
            step_f[h][j].wait_send()
        for j in range(2):
            low_step_f[h][j].wait_send()


def reduce_blocks(sent_act, sent_grad, embedded, loss_grad, micro_weight, order):
    dma = pltpu.SemaphoreType.DMA
    block = (TOP + 8, BLK)
    pair = (2 * TOP + 8, BLK)
    low = (2, LOW, BLK)
    hbm, smem = pl.BlockSpec(memory_space=pltpu.HBM), pl.BlockSpec(memory_space=pltpu.SMEM)
    return pl.pallas_call(
        reduce_kernel,
        out_shape=jax.ShapeDtypeStruct((2, PACKED, BLK), jnp.float32),
        in_specs=[hbm] * 4 + [smem] * 2,
        out_specs=pl.BlockSpec(memory_space=pltpu.VMEM),
        scratch_shapes=[
            pltpu.VMEM((ROWS, 2 * D), jnp.bfloat16),
            pltpu.VMEM((2, SIDE) + pair, jnp.float32),
            pltpu.VMEM((2, SIDE, 2) + block, jnp.float32),
            pltpu.VMEM((2, SIDE) + pair, jnp.float32),
            pltpu.VMEM((2, SIDE) + block, jnp.float32),
            pltpu.VMEM((2,) + block, jnp.float32),
            pltpu.VMEM((2, 3) + block, jnp.float32),
            pltpu.VMEM((2, SIDE) + low, jnp.float32),
            pltpu.VMEM((2, SIDE) + low, jnp.float32),
            pltpu.VMEM((2, SIDE) + low, jnp.float32),
            pltpu.VMEM((2, 2) + low, jnp.float32),
            pltpu.VMEM((2,) + low, jnp.float32),
            pltpu.VMEM((2,) + low, jnp.float32),
            dma((SIDE, SIDE)),
            dma((2, SIDE)), dma((2, SIDE)), dma((2, SIDE)), dma((2, SIDE)),
            dma((2,)), dma((2,)), dma((2, 3)), dma((2, 3)),
            dma((2, SIDE)), dma((2, SIDE)), dma((2, 2)), dma((2, 2)),
            dma((2,)), dma((2,)), dma((2, 2)), dma((2, 2)),
        ],
        compiler_params=pltpu.CompilerParams(
            collective_id=0, has_side_effects=True, vmem_limit_bytes=VMEM_LIMIT
        ),
        name="gram_reduce",
    )(sent_act, sent_grad, embedded, loss_grad, micro_weight, order)


def split3(x):
    high = x.astype(jnp.bfloat16)
    rest = x - high.astype(jnp.float32)
    middle = rest.astype(jnp.bfloat16)
    low = (rest - middle.astype(jnp.float32)).astype(jnp.bfloat16)
    return high, middle, low


def dot(x, y):
    return lax.dot_general(x, y, (((1,), (0,)), ((), ())), preferred_element_type=jnp.float32)


def narrow(x):
    return x.astype(jnp.bfloat16)


def total(x):
    return jnp.sum(jnp.sum(x, axis=0, keepdims=True), axis=1, keepdims=True)


def dot_exact(x, y):
    h0, m0, l0 = split3(x)
    h1, m1, l1 = split3(y)
    left = jnp.concatenate([l0, h0, m0, m0, h0, h0], axis=1)
    right = jnp.concatenate([h1, l1, m1, h1, m1, h1], axis=0)
    return dot(left, right)


def sweep(work):
    sub = lax.broadcasted_iota(jnp.int32, (PANEL, BLK), 0)
    lane = lax.broadcasted_iota(jnp.int32, (PANEL, BLK), 1)
    col_at = lax.broadcasted_iota(jnp.int32, (BLK, BLK), 1)

    def spread_row(x, k):
        return jnp.broadcast_to(x[k:k + 1, :], (PANEL, BLK))

    for p in range(BLK // PANEL):
        start = p * PANEL
        inside = (lane >= start) & (lane < start + PANEL)
        panel_cols = (col_at >= start) & (col_at < start + PANEL)
        original = [work[m, start:start + PANEL, :] for m in range(OWN)]
        state = list(original)
        columns = [
            [jnp.broadcast_to(x[:, start + j:start + j + 1], (PANEL, BLK)) for j in range(PANEL)]
            for x in original
        ]
        for k in range(PANEL):
            for m in range(OWN):
                here = columns[m][k]
                inverse = 1.0 / spread_row(here, k)
                marked = jnp.where(lane == start + k, jnp.where(sub == k, 1.0, 0.0), state[m])
                pivot_row = spread_row(marked, k) * inverse
                state[m] = jnp.where(sub == k, pivot_row, marked - here * pivot_row)
                for j in range(k + 1, PANEL):
                    step = spread_row(columns[m][j], k) * inverse
                    columns[m][j] = jnp.where(sub == k, step, columns[m][j] - here * step)
        for m in range(OWN):
            swept = jnp.where(inside, -state[m], state[m])
            h0, m0, l0 = split3(original[m])
            h1, m1, l1 = split3(swept)
            left = jnp.concatenate([h0, h0, m0, m0, h0, l0], axis=0)
            right = jnp.concatenate([h1, m1, h1, m1, l1, h1], axis=0)
            update = lax.dot_general(
                left, right, (((0,), (0,)), ((), ())), preferred_element_type=jnp.float32
            )
            work[m] = jnp.where(panel_cols, 0.0, work[m]) - update
            work[m, start:start + PANEL, :] = swept


def invert_kernel(micro_weight, assignment, packed, old_hbm, out_hbm, work, old, out, mask, sems):
    r = lax.axis_index("dp")
    get_old = pltpu.make_async_copy(old_hbm, old, sems.at[0])
    get_mask = pltpu.make_async_copy(assignment, mask, sems.at[1])
    get_old.start()
    get_mask.start()
    row_at = lax.broadcasted_iota(jnp.int32, (BLK, BLK), 0)
    col_at = lax.broadcasted_iota(jnp.int32, (BLK, BLK), 1)
    on_diagonal = row_at == col_at
    identity = jnp.where(on_diagonal, 1.0, 0.0)
    scale = 1.0 / (MROWS * total(micro_weight[...]))
    for half in range(2):
        square = packed[half, :BLK, :]
        flipped = square.T
        one = jnp.where(row_at >= col_at, square, flipped)
        two = jnp.where(row_at < col_at, square, flipped)
        two = jnp.where(on_diagonal, packed[half, BLK:BLK + 1, :], two)
        work[2 * half] = one * scale + damping * identity
        work[2 * half + 1] = two * scale + damping * identity

    every = range(OWN)
    factors = [work[m] for m in every]
    spots = [jnp.where(on_diagonal, x, 0.0) for x in factors]
    along = [lax.rsqrt(jnp.sum(x, axis=0, keepdims=True)) for x in spots]
    down = [lax.rsqrt(jnp.sum(x, axis=1, keepdims=True)) for x in spots]
    unit = [factors[m] * along[m] * down[m] for m in every]
    gains = [BLK / total(x * x) for x in unit]
    power = [identity - gains[m] * unit[m] for m in every]
    series = [identity + x for x in power]
    power = [dot(narrow(x), narrow(x)) for x in power]
    for _ in range(ROUNDS):
        both = [
            dot(narrow(power[m]),
                jnp.concatenate([narrow(power[m]), narrow(series[m])], axis=1)) for m in every
        ]
        series = [series[m] + both[m][:, BLK:] for m in every]
        power = [x[:, :BLK] for x in both]
    series = [series[m] + dot(narrow(power[m]), narrow(series[m])) for m in every]
    guess = [gains[m] * series[m] for m in every]
    rest = [identity - dot_exact(unit[m], guess[m]) for m in every]
    square = [dot(narrow(x), narrow(x)) for x in rest]
    size = [total(x * x) for x in square]
    worst = jnp.maximum(jnp.maximum(size[0], size[1]), jnp.maximum(size[2], size[3]))
    square = [square[m] + dot(narrow(square[m]), narrow(rest[m])) for m in every]
    change = [rest[m] + square[m] for m in every]
    fresh = [guess[m] + dot_exact(guess[m], change[m]) for m in every]
    for m in every:
        out[0, m] = fresh[m] * along[m] * down[m]

    @pl.when(jnp.logical_not(worst[0, 0] <= LIMIT))
    def _():
        sweep(work)
        for m in every:
            out[0, m] = -work[m]

    get_old.wait()
    get_mask.wait()
    puts = []
    for m in every:
        refreshed = mask[0, r * OWN + m] < REPLICAS
        out[0, m] = jnp.where(refreshed, out[0, m], old[0, m])
        puts.append(pltpu.make_async_copy(out.at[0, m], out_hbm.at[0, m], sems.at[2 + m]))
        puts[m].start()
    for put in puts:
        put.wait()


def invert_blocks(micro_weight, assignment, packed, old_inverse):
    vmem, hbm = pl.BlockSpec(memory_space=pltpu.VMEM), pl.BlockSpec(memory_space=pltpu.HBM)
    return pl.pallas_call(
        invert_kernel,
        out_shape=jax.ShapeDtypeStruct(old_inverse.shape, jnp.float32),
        in_specs=[vmem, hbm, vmem, hbm],
        out_specs=hbm,
        scratch_shapes=[
            pltpu.VMEM((OWN, BLK, BLK), jnp.float32),
            pltpu.VMEM((1, OWN, BLK, BLK), jnp.float32),
            pltpu.VMEM((1, OWN, BLK, BLK), jnp.float32),
            pltpu.SMEM((1, NBLK), jnp.int32),
            pltpu.SemaphoreType.DMA((2 + OWN,)),
        ],
        compiler_params=pltpu.CompilerParams(vmem_limit_bytes=VMEM_LIMIT),
        name="invert",
    )(micro_weight, assignment, packed, old_inverse)


def shards(sent_act, sent_grad, embedded, loss_grad, micro_weight, order, assignment, old_inverse):
    micro_weight = micro_weight.T
    packed = reduce_blocks(sent_act, sent_grad, embedded, loss_grad, micro_weight, order.T)
    return invert_blocks(micro_weight, assignment, packed, old_inverse)


def solution(mesh):
    in_specs = (
        P("section", "dp", None),
        P("section", "dp", None),
        P("dp", None),
        P("dp", None),
        P(),
        P(),
        P("section", None),
        P("section", "dp", None, None),
    )
    out_specs = P("section", "dp", None, None)
    return jax.shard_map(shards, mesh=mesh, in_specs=in_specs, out_specs=out_specs, check_vma=False)
```

```python
import jax
import jax.numpy as jnp
from jax import lax
from jax.experimental import pallas as pl
from jax.experimental.pallas import tpu as pltpu
from jax.sharding import PartitionSpec as P

D = 4096
BLK = 128
MB = 4
MROWS = 64
ROWS = MB * MROWS
NBLK = 64
OWN = 4
SIDE = 4
SECTIONS = 16
REPLICAS = 16
PACKED = BLK + 8
QUARTER = BLK // 4
CODED = 3 * QUARTER
BITS = 22.0
GROUPS = ((0,), (1,), (2,), (3,))


def message_rows(units):
    return units * CODED + -(-3 * units // 8) * 8


GIVE_AT = [sum(message_rows(2 * len(g)) for g in GROUPS[:i]) for i in range(len(GROUPS) + 1)]
PASS_AT = [sum(message_rows(len(g)) for g in GROUPS[:i]) for i in range(len(GROUPS) + 1)]
PANEL = 8
ROUNDS = 2
LIMIT = 1e-6
VMEM_LIMIT = 60 * 1024 * 1024
MESH = pl.DeviceIdType.MESH

damping = 0.1


def flip1(v):
    return v + 1 - 2 * (v % 2)


def flip2(v):
    return (v + 2) % 4


def flip3(v):
    return 3 - v


def spread(v, half):
    if half == 0:
        return flip2(v), flip1(v), flip3(v), v
    return flip2(v), flip3(v), flip1(v), v


def final_target(s, y):
    low, last, inner = 1 - y // 2, s // (SECTIONS - 1), (s + SECTIONS - 1) // SECTIONS
    to_s = s + low * (1 - last) - (1 - low) * inner
    to_y = y + 2 * low * last - 2 * (1 - low) * (1 - inner)
    return to_s, to_y


def final_source(s, y):
    low, last, inner = 1 - y // 2, s // (SECTIONS - 1), (s + SECTIONS - 1) // SECTIONS
    from_s = s - low * inner + (1 - low) * (1 - last)
    from_y = y + 2 * low * (1 - inner) - 2 * (1 - low) * last
    return from_s, from_y


def encode(square, diagonal, row_at, col_at):
    first = jnp.sum(jnp.where(row_at == col_at, square, 0.0), axis=0, keepdims=True)
    marks = []
    for entry in (first, diagonal):
        entry = jnp.maximum(entry, 1e-30)
        largest = jnp.max(entry, axis=1, keepdims=True)
        marks.append(jnp.ceil(0.5 * (jnp.log2(entry) + jnp.log2(largest))))
    gain = [jnp.exp2(BITS - mark) for mark in marks]
    values = (square * jnp.where(row_at >= col_at, gain[0], gain[1])).astype(jnp.int32)
    part = [values[i * QUARTER:(i + 1) * QUARTER] for i in range(4)]
    words = [(part[i] << 8) | ((part[3] >> (8 * i)) & 255) for i in range(3)]
    fine = (diagonal * (gain[1] * 256.0)).astype(jnp.int32)
    return (jnp.concatenate(words, axis=0),
            (marks[0].astype(jnp.int32), marks[1].astype(jnp.int32), fine))


def decode(words, marks, row_at, col_at):
    part = [words[i * QUARTER:(i + 1) * QUARTER] for i in range(3)]
    last = (part[0] & 255) | ((part[1] & 255) << 8) | ((part[2] & 255) << 16)
    values = jnp.concatenate([x >> 8 for x in part] + [(last << 8) >> 8], axis=0)
    step = [jnp.exp2(mark.astype(jnp.float32) - BITS) for mark in marks[:2]]
    square = values.astype(jnp.float32) * jnp.where(row_at >= col_at, step[0], step[1])
    return square, marks[2].astype(jnp.float32) * (step[1] * (1.0 / 256.0))


def reduce_kernel(
    sent_act, sent_grad, embedded, loss_grad, micro_weight, order, out,
    rows, give, pass_on, coded, keep, got_y1, got_y2, got_z1, got_f,
    weight_table, order_table, in_sem, table_sem,
    y1_send, y1_recv, y2_send, y2_recv, z1_send, z1_recv, f_send, f_recv,
):
    s = lax.axis_index("section")
    r = lax.axis_index("dp")
    y, z = r // SIDE, r % SIDE

    barrier = pltpu.get_barrier_semaphore()
    from_s, from_y = final_source(s, y)
    greet = [(s, flip1(y), z), (s, flip3(y), z), (s, y, flip1(z)), (s, y, flip3(z))]
    greet += [(from_s, from_y, z), (from_s, from_y, flip1(z)), (from_s, from_y, flip3(z))]
    for to_s, to_y, to_z in greet:
        pl.semaphore_signal(
            barrier, inc=1, device_id=(to_s, to_y * SIDE + to_z), device_id_type=MESH
        )

    tables = [
        pltpu.make_async_copy(micro_weight, weight_table, table_sem.at[0]),
        pltpu.make_async_copy(order, order_table, table_sem.at[1]),
    ]

    def fetch(src, to_y, place):
        pair = (z // 2 + 1 + place) % 2
        column = (to_y * SIDE + pair * 2) * OWN * BLK
        wide = pl.ds(pl.multiple_of(column, 2 * OWN * BLK), 2 * OWN * BLK)
        narrow = pl.ds(pl.multiple_of(column - to_y // 2 * D, 2 * OWN * BLK), 2 * OWN * BLK)
        return pltpu.make_async_copy(
            src.at[:, narrow], rows.at[:, wide], in_sem.at[place, to_y]
        )

    for place in range(2):
        @pl.when(s < SECTIONS - 1)
        def _():
            for to_y in range(2):
                fetch(sent_act.at[0], to_y, place).start()

        @pl.when(s == SECTIONS - 1)
        def _():
            for to_y in range(2):
                fetch(loss_grad, to_y, place).start()

        @pl.when(s > 0)
        def _():
            for to_y in range(2, 4):
                fetch(sent_grad.at[0], to_y, place).start()

        @pl.when(s == 0)
        def _():
            for to_y in range(2, 4):
                fetch(embedded, to_y, place).start()

        if place == 0:
            for table in tables:
                table.start()

    def fetched(place):
        for to_y in range(SIDE):
            fetch(sent_act.at[0], to_y, place).wait()

    for table in tables:
        table.wait()
    weights = []
    for slot in range(MB):
        batch = order_table[slot, s]
        weight = jnp.float32(0.0)
        for m in range(MB):
            weight = weight + jnp.where(batch == m, weight_table[m, r], 0.0)
        weights.append(weight)

    row_at = lax.broadcasted_iota(jnp.int32, (BLK, BLK), 0)
    col_at = lax.broadcasted_iota(jnp.int32, (BLK, BLK), 1)
    blank = jnp.zeros((MROWS, BLK), jnp.bfloat16)
    y_orders, z_orders = [spread(y, h) for h in range(2)], [spread(z, h) for h in range(2)]

    def unit(half, y_at, z_at):
        column = ((y_at * SIDE + z_at) * OWN + 2 * half) * BLK
        total = None
        for slot in range(MB):
            at = pl.ds(slot * MROWS, MROWS)
            one = rows[at, pl.ds(pl.multiple_of(column, 2 * BLK), BLK)]
            two = rows[at, pl.ds(pl.multiple_of(column + BLK, BLK), BLK)]
            left = jnp.concatenate([one, two], axis=0)
            right = jnp.concatenate(
                [jnp.concatenate([one, blank], axis=1), jnp.concatenate([blank, two], axis=1)],
                axis=0,
            )
            term = weights[slot] * lax.dot_general(
                left, right, (((0,), (0,)), ((), ())), preferred_element_type=jnp.float32
            )
            total = term if total is None else total + term
        first, second = total[:, :BLK], total[:, BLK:]
        square = jnp.where(row_at >= col_at, first, second)
        diagonal = jnp.sum(jnp.where(row_at == col_at, second, 0.0), axis=0, keepdims=True)
        return square, diagonal

    def compute(chunk):
        group = [g for g in range(len(GROUPS)) if chunk in GROUPS[g]][0]
        size, at = len(GROUPS[group]), GROUPS[group].index(chunk)
        for half in range(2):
            for i in range(SIDE):
                square, diagonal = unit(half, y_orders[half][i], z_orders[half][chunk])
                if i < 2:
                    words, marks = encode(square, diagonal, row_at, col_at)
                    row = GIVE_AT[group] + (i * size + at) * CODED
                    give[half, row:row + CODED, :] = words
                    row = GIVE_AT[group] + 2 * size * CODED + 3 * (i * size + at)
                    for mark in marks:
                        give[half, row:row + 1, :] = mark
                        row += 1
                elif i == 2:
                    pass_on[half, chunk, :BLK, :] = square
                    pass_on[half, chunk, BLK:, :] = jnp.broadcast_to(diagonal, (8, BLK))
                else:
                    keep[half, chunk, :BLK, :] = square
                    keep[half, chunk, BLK:, :] = jnp.broadcast_to(diagonal, (8, BLK))

    def remote(src, dst, send, recv, to):
        return pltpu.make_async_remote_copy(
            src_ref=src, dst_ref=dst, send_sem=send, recv_sem=recv,
            device_id=(to[0], to[1] * SIDE + to[2]), device_id_type=MESH,
        )

    y_first = [flip1(y), flip3(y)]
    y_second = [flip3(y), flip1(y)]
    z_first = [flip1(z), flip3(z)]
    z_second = [flip3(z), flip1(z)]
    to_s, to_y = final_target(s, y)
    halves, chunks, groups = range(2), range(SIDE), range(len(GROUPS))

    def give_part(ref, h, g):
        return ref.at[h, pl.ds(GIVE_AT[g], GIVE_AT[g + 1] - GIVE_AT[g])]

    def pass_part(ref, h, g):
        return ref.at[h, pl.ds(PASS_AT[g], PASS_AT[g + 1] - PASS_AT[g])]

    step_y1 = [[remote(give_part(give, h, g), give_part(got_y1, h, g), y1_send.at[h, g],
                       y1_recv.at[h, g], (s, y_first[h], z)) for g in groups] for h in halves]
    step_y2 = [[remote(pass_part(coded, h, g), pass_part(got_y2, h, g), y2_send.at[h, g],
                       y2_recv.at[h, g], (s, y_second[h], z)) for g in groups] for h in halves]
    step_z1 = [remote(keep.at[h, 0], got_z1.at[h], z1_send.at[h], z1_recv.at[h],
                      (s, y, z_first[h])) for h in halves]
    step_f = [[remote(keep.at[h, 1 + j], got_f.at[h, j], f_send.at[h, j], f_recv.at[h, j],
                      (to_s, to_y, to_z))
               for j, to_z in enumerate((z_first[h], z_second[h], z))] for h in halves]
    def start_y1(g):
        for h in halves:
            step_y1[h][g].start()

    def add_coded(ref, h, c, got, words_at, marks_at):
        words = got[h, words_at:words_at + CODED]
        marks = [got[h, marks_at + i:marks_at + i + 1] for i in range(3)]
        square, diagonal = decode(words, marks, row_at, col_at)
        ref[h, c, :BLK] = ref[h, c, :BLK] + square
        ref[h, c, BLK:BLK + 1] = ref[h, c, BLK:BLK + 1] + diagonal

    def after_y1(g):
        size, base, mine = len(GROUPS[g]), GIVE_AT[g], PASS_AT[g]
        marks = base + 2 * size * CODED
        for h in halves:
            step_y1[h][g].wait_recv()
            for at in range(size):
                c = GROUPS[g][at]
                add_coded(pass_on, h, c, got_y1, base + at * CODED, marks + 3 * at)
                words, extra = encode(
                    pass_on[h, c, :BLK], pass_on[h, c, BLK:BLK + 1], row_at, col_at
                )
                row = mine + at * CODED
                coded[h, row:row + CODED] = words
                row = mine + size * CODED + 3 * at
                for mark in extra:
                    coded[h, row:row + 1] = mark
                    row += 1
            step_y2[h][g].start()
        for h in halves:
            for at in range(size):
                c, place = GROUPS[g][at], size + at
                add_coded(keep, h, c, got_y1, base + place * CODED, marks + 3 * place)

    def after_y2(g):
        size = len(GROUPS[g])
        for h in halves:
            step_y2[h][g].wait_recv()
            for at in range(size):
                c, base = GROUPS[g][at], PASS_AT[g]
                add_coded(keep, h, c, got_y2, base + at * CODED, base + size * CODED + 3 * at)
                if c == 2:
                    step_z1[h].wait_recv()
                    keep[h, c] = keep[h, c] + got_z1[h]
                (step_z1[h] if c == 0 else step_f[h][c - 1]).start()

    fetched(0)
    compute(0)
    pl.semaphore_wait(barrier, len(greet))
    start_y1(0)
    fetched(1)
    compute(1)
    start_y1(1)
    compute(2)
    compute(3)
    after_y1(0)
    start_y1(2)
    after_y1(1)
    start_y1(3)
    after_y2(0)
    after_y1(2)
    after_y2(1)
    after_y1(3)
    after_y2(2)
    after_y2(3)
    weight_sum = jnp.float32(0.0)
    for m in range(MB):
        for other in range(REPLICAS):
            weight_sum = weight_sum + weight_table[m, other]
    shrink = 1.0 / (MROWS * jnp.full((8, BLK), weight_sum))[:1]
    for h in halves:
        for g in groups:
            step_y1[h][g].wait_send()
            step_y2[h][g].wait_send()
        step_z1[h].wait_send()
    for h in halves:
        for j in range(3):
            step_f[h][j].wait_recv()
        out[h] = (got_f[h, 0] + got_f[h, 1] + got_f[h, 2]) * shrink
    for h in halves:
        for j in range(3):
            step_f[h][j].wait_send()


def reduce_blocks(sent_act, sent_grad, embedded, loss_grad, micro_weight, order):
    dma = pltpu.SemaphoreType.DMA
    block = (PACKED, BLK)
    given, passed = (2, GIVE_AT[-1], BLK), (2, PASS_AT[-1], BLK)
    count = len(GROUPS)
    hbm = pl.BlockSpec(memory_space=pltpu.HBM)
    return pl.pallas_call(
        reduce_kernel,
        out_shape=jax.ShapeDtypeStruct((2, PACKED, BLK), jnp.float32),
        in_specs=[hbm] * 6,
        out_specs=pl.BlockSpec(memory_space=pltpu.VMEM),
        scratch_shapes=[
            pltpu.VMEM((ROWS, 2 * D), jnp.bfloat16),
            pltpu.VMEM(given, jnp.int32),
            pltpu.VMEM((2, SIDE) + block, jnp.float32),
            pltpu.VMEM(passed, jnp.int32),
            pltpu.VMEM((2, SIDE) + block, jnp.float32),
            pltpu.VMEM(given, jnp.int32),
            pltpu.VMEM(passed, jnp.int32),
            pltpu.VMEM((2,) + block, jnp.float32),
            pltpu.VMEM((2, 3) + block, jnp.float32),
            pltpu.SMEM((MB, REPLICAS), jnp.float32),
            pltpu.SMEM((MB, SECTIONS), jnp.int32),
            dma((2, SIDE)), dma((2,)),
            dma((2, count)), dma((2, count)), dma((2, count)), dma((2, count)),
            dma((2,)), dma((2,)), dma((2, 3)), dma((2, 3)),
        ],
        compiler_params=pltpu.CompilerParams(
            collective_id=0, has_side_effects=True, vmem_limit_bytes=VMEM_LIMIT
        ),
        name="gram_reduce",
    )(sent_act, sent_grad, embedded, loss_grad, micro_weight, order)


def split3(x):
    high = x.astype(jnp.bfloat16)
    rest = x - high.astype(jnp.float32)
    middle = rest.astype(jnp.bfloat16)
    low = (rest - middle.astype(jnp.float32)).astype(jnp.bfloat16)
    return high, middle, low


def dot(x, y):
    return lax.dot_general(x, y, (((1,), (0,)), ((), ())), preferred_element_type=jnp.float32)


def narrow(x):
    return x.astype(jnp.bfloat16)


def total(x):
    return jnp.sum(jnp.sum(x, axis=0, keepdims=True), axis=1, keepdims=True)


def dot_exact(x, y):
    h0, m0, l0 = split3(x)
    h1, m1, l1 = split3(y)
    left = jnp.concatenate([l0, h0, m0, m0, h0, h0], axis=1)
    right = jnp.concatenate([h1, l1, m1, h1, m1, h1], axis=0)
    return dot(left, right)


def sweep(work):
    sub = lax.broadcasted_iota(jnp.int32, (PANEL, BLK), 0)
    lane = lax.broadcasted_iota(jnp.int32, (PANEL, BLK), 1)
    col_at = lax.broadcasted_iota(jnp.int32, (BLK, BLK), 1)

    def spread_row(x, k):
        return jnp.broadcast_to(x[k:k + 1, :], (PANEL, BLK))

    for p in range(BLK // PANEL):
        start = p * PANEL
        inside = (lane >= start) & (lane < start + PANEL)
        panel_cols = (col_at >= start) & (col_at < start + PANEL)
        original = [work[m, start:start + PANEL, :] for m in range(OWN)]
        state = list(original)
        columns = [
            [jnp.broadcast_to(x[:, start + j:start + j + 1], (PANEL, BLK)) for j in range(PANEL)]
            for x in original
        ]
        for k in range(PANEL):
            for m in range(OWN):
                here = columns[m][k]
                inverse = 1.0 / spread_row(here, k)
                marked = jnp.where(lane == start + k, jnp.where(sub == k, 1.0, 0.0), state[m])
                pivot_row = spread_row(marked, k) * inverse
                state[m] = jnp.where(sub == k, pivot_row, marked - here * pivot_row)
                for j in range(k + 1, PANEL):
                    step = spread_row(columns[m][j], k) * inverse
                    columns[m][j] = jnp.where(sub == k, step, columns[m][j] - here * step)
        for m in range(OWN):
            swept = jnp.where(inside, -state[m], state[m])
            h0, m0, l0 = split3(original[m])
            h1, m1, l1 = split3(swept)
            left = jnp.concatenate([h0, h0, m0, m0, h0, l0], axis=0)
            right = jnp.concatenate([h1, m1, h1, m1, l1, h1], axis=0)
            update = lax.dot_general(
                left, right, (((0,), (0,)), ((), ())), preferred_element_type=jnp.float32
            )
            work[m] = jnp.where(panel_cols, 0.0, work[m]) - update
            work[m, start:start + PANEL, :] = swept


def invert_kernel(assignment, packed, old_hbm, out_hbm, work, old, out, mask, sems):
    r = lax.axis_index("dp")
    get_old = pltpu.make_async_copy(old_hbm, old, sems.at[0])
    get_mask = pltpu.make_async_copy(assignment, mask, sems.at[1])
    get_old.start()
    get_mask.start()
    row_at = lax.broadcasted_iota(jnp.int32, (BLK, BLK), 0)
    col_at = lax.broadcasted_iota(jnp.int32, (BLK, BLK), 1)
    on_diagonal = row_at == col_at
    identity = jnp.where(on_diagonal, 1.0, 0.0)
    for half in range(2):
        square = packed[half, :BLK, :]
        flipped = square.T
        one = jnp.where(row_at >= col_at, square, flipped)
        two = jnp.where(row_at < col_at, square, flipped)
        two = jnp.where(on_diagonal, packed[half, BLK:BLK + 1, :], two)
        work[2 * half] = one + damping * identity
        work[2 * half + 1] = two + damping * identity

    every = range(OWN)
    factors = [work[m] for m in every]
    spots = [jnp.where(on_diagonal, x, 0.0) for x in factors]
    along = [lax.rsqrt(jnp.sum(x, axis=0, keepdims=True)) for x in spots]
    down = [lax.rsqrt(jnp.sum(x, axis=1, keepdims=True)) for x in spots]
    unit = [factors[m] * along[m] * down[m] for m in every]
    gains = [BLK / total(x * x) for x in unit]
    power = [identity - gains[m] * unit[m] for m in every]
    series = [identity + x for x in power]
    power = [dot(narrow(x), narrow(x)) for x in power]
    for _ in range(ROUNDS):
        both = [
            dot(narrow(power[m]),
                jnp.concatenate([narrow(power[m]), narrow(series[m])], axis=1)) for m in every
        ]
        series = [series[m] + both[m][:, BLK:] for m in every]
        power = [x[:, :BLK] for x in both]
    series = [series[m] + dot(narrow(power[m]), narrow(series[m])) for m in every]
    guess = [gains[m] * series[m] for m in every]
    rest = [identity - dot_exact(unit[m], guess[m]) for m in every]
    square = [dot(narrow(x), narrow(x)) for x in rest]
    size = [total(x * x) for x in square]
    worst = jnp.maximum(jnp.maximum(size[0], size[1]), jnp.maximum(size[2], size[3]))
    square = [square[m] + dot(narrow(square[m]), narrow(rest[m])) for m in every]
    change = [rest[m] + square[m] for m in every]
    fresh = [guess[m] + dot_exact(guess[m], change[m]) for m in every]
    for m in every:
        out[0, m] = fresh[m] * along[m] * down[m]

    @pl.when(jnp.logical_not(worst[0, 0] <= LIMIT))
    def _():
        sweep(work)
        for m in every:
            out[0, m] = -work[m]

    get_old.wait()
    get_mask.wait()
    puts = []
    for m in every:
        refreshed = mask[0, r * OWN + m] < REPLICAS
        out[0, m] = jnp.where(refreshed, out[0, m], old[0, m])
        puts.append(pltpu.make_async_copy(out.at[0, m], out_hbm.at[0, m], sems.at[2 + m]))
        puts[m].start()
    for put in puts:
        put.wait()


def invert_blocks(assignment, packed, old_inverse):
    vmem, hbm = pl.BlockSpec(memory_space=pltpu.VMEM), pl.BlockSpec(memory_space=pltpu.HBM)
    return pl.pallas_call(
        invert_kernel,
        out_shape=jax.ShapeDtypeStruct(old_inverse.shape, jnp.float32),
        in_specs=[hbm, vmem, hbm],
        out_specs=hbm,
        scratch_shapes=[
            pltpu.VMEM((OWN, BLK, BLK), jnp.float32),
            pltpu.VMEM((1, OWN, BLK, BLK), jnp.float32),
            pltpu.VMEM((1, OWN, BLK, BLK), jnp.float32),
            pltpu.SMEM((1, NBLK), jnp.int32),
            pltpu.SemaphoreType.DMA((2 + OWN,)),
        ],
        compiler_params=pltpu.CompilerParams(vmem_limit_bytes=VMEM_LIMIT),
        name="invert",
    )(assignment, packed, old_inverse)


def shards(sent_act, sent_grad, embedded, loss_grad, micro_weight, order, assignment, old_inverse):
    packed = reduce_blocks(sent_act, sent_grad, embedded, loss_grad, micro_weight.T, order.T)
    return invert_blocks(assignment, packed, old_inverse)


def solution(mesh):
    in_specs = (
        P("section", "dp", None),
        P("section", "dp", None),
        P("dp", None),
        P("dp", None),
        P(),
        P(),
        P("section", None),
        P("section", "dp", None, None),
    )
    out_specs = P("section", "dp", None, None)
    return jax.shard_map(shards, mesh=mesh, in_specs=in_specs, out_specs=out_specs, check_vma=False)
```

```python
import jax
import jax.numpy as jnp
from jax import lax
from jax.experimental import pallas as pl
from jax.experimental.pallas import tpu as pltpu
from jax.sharding import PartitionSpec as P

D = 4096
BLK = 128
MB = 4
MROWS = 64
ROWS = MB * MROWS
NBLK = 64
OWN = 4
SIDE = 4
SECTIONS = 16
REPLICAS = 16
PACKED = BLK + 8
QUARTER = BLK // 4
CODED = 3 * QUARTER
BITS = 22.0
PANEL = 8
ROUNDS = 2
LIMIT = 1e-6
VMEM_LIMIT = 60 * 1024 * 1024
MESH = pl.DeviceIdType.MESH

damping = 0.1


def flip1(v):
    return v + 1 - 2 * (v % 2)


def flip2(v):
    return (v + 2) % 4


def flip3(v):
    return 3 - v


def spread(v, half):
    if half == 0:
        return flip2(v), flip1(v), flip3(v), v
    return flip2(v), flip3(v), flip1(v), v


def final_target(s, y):
    low, last, inner = 1 - y // 2, s // (SECTIONS - 1), (s + SECTIONS - 1) // SECTIONS
    to_s = s + low * (1 - last) - (1 - low) * inner
    to_y = y + 2 * low * last - 2 * (1 - low) * (1 - inner)
    return to_s, to_y


def final_source(s, y):
    low, last, inner = 1 - y // 2, s // (SECTIONS - 1), (s + SECTIONS - 1) // SECTIONS
    from_s = s - low * inner + (1 - low) * (1 - last)
    from_y = y + 2 * low * (1 - inner) - 2 * (1 - low) * last
    return from_s, from_y


def encode(square, diagonal, row_at, col_at):
    first = jnp.sum(jnp.where(row_at == col_at, square, 0.0), axis=0, keepdims=True)
    marks = []
    for entry in (first, diagonal):
        entry = jnp.maximum(entry, 1e-30)
        largest = jnp.max(entry, axis=1, keepdims=True)
        marks.append(jnp.ceil(0.5 * (jnp.log2(entry) + jnp.log2(largest))))
    gain = [jnp.exp2(BITS - mark) for mark in marks]
    values = (square * jnp.where(row_at >= col_at, gain[0], gain[1])).astype(jnp.int32)
    part = [values[i * QUARTER:(i + 1) * QUARTER] for i in range(4)]
    words = [(part[i] << 8) | ((part[3] >> (8 * i)) & 255) for i in range(3)]
    fine = (diagonal * (gain[1] * 256.0)).astype(jnp.int32)
    return (jnp.concatenate(words, axis=0),
            (marks[0].astype(jnp.int32), marks[1].astype(jnp.int32), fine))


def decode(words, marks, row_at, col_at):
    part = [words[i * QUARTER:(i + 1) * QUARTER] for i in range(3)]
    last = (part[0] & 255) | ((part[1] & 255) << 8) | ((part[2] & 255) << 16)
    values = jnp.concatenate([x >> 8 for x in part] + [(last << 8) >> 8], axis=0)
    step = [jnp.exp2(mark.astype(jnp.float32) - BITS) for mark in marks[:2]]
    square = values.astype(jnp.float32) * jnp.where(row_at >= col_at, step[0], step[1])
    return square, marks[2].astype(jnp.float32) * (step[1] * (1.0 / 256.0))


def reduce_kernel(
    sent_act, sent_grad, embedded, loss_grad, micro_weight, order, out,
    rows, give, pass_on, coded, keep, got_y1, got_y2, got_z1, got_f,
    weight_table, order_table, in_sem, table_sem,
    y1_send, y1_recv, y2_send, y2_recv, z1_send, z1_recv, f_send, f_recv,
):
    s = lax.axis_index("section")
    r = lax.axis_index("dp")
    y, z = r // SIDE, r % SIDE

    barrier = pltpu.get_barrier_semaphore()
    from_s, from_y = final_source(s, y)
    greet = [(s, flip1(y), z), (s, flip3(y), z), (s, y, flip1(z)), (s, y, flip3(z))]
    greet += [(from_s, from_y, z), (from_s, from_y, flip1(z)), (from_s, from_y, flip3(z))]
    for to_s, to_y, to_z in greet:
        pl.semaphore_signal(
            barrier, inc=1, device_id=(to_s, to_y * SIDE + to_z), device_id_type=MESH
        )

    tables = [
        pltpu.make_async_copy(micro_weight, weight_table, table_sem.at[0]),
        pltpu.make_async_copy(order, order_table, table_sem.at[1]),
    ]

    def fetch(src, to_y, place):
        pair = (z // 2 + 1 + place) % 2
        column = (to_y * SIDE + pair * 2) * OWN * BLK
        wide = pl.ds(pl.multiple_of(column, 2 * OWN * BLK), 2 * OWN * BLK)
        narrow = pl.ds(pl.multiple_of(column - to_y // 2 * D, 2 * OWN * BLK), 2 * OWN * BLK)
        return pltpu.make_async_copy(
            src.at[:, narrow], rows.at[:, wide], in_sem.at[place]
        )

    for place in range(2):
        @pl.when(s < SECTIONS - 1)
        def _():
            for to_y in range(2):
                fetch(sent_act.at[0], to_y, place).start()

        @pl.when(s == SECTIONS - 1)
        def _():
            for to_y in range(2):
                fetch(loss_grad, to_y, place).start()

        @pl.when(s > 0)
        def _():
            for to_y in range(2, 4):
                fetch(sent_grad.at[0], to_y, place).start()

        @pl.when(s == 0)
        def _():
            for to_y in range(2, 4):
                fetch(embedded, to_y, place).start()

        if place == 0:
            for table in tables:
                table.start()

    def fetched(place):
        pltpu.make_async_copy(sent_act.at[0], rows.at[:, pl.ds(0, D)], in_sem.at[place]).wait()

    for table in tables:
        table.wait()
    weights = []
    for slot in range(MB):
        batch = order_table[slot, s]
        weight = jnp.float32(0.0)
        for m in range(MB):
            weight = weight + jnp.where(batch == m, weight_table[m, r], 0.0)
        weights.append(weight)

    row_at = lax.broadcasted_iota(jnp.int32, (BLK, BLK), 0)
    col_at = lax.broadcasted_iota(jnp.int32, (BLK, BLK), 1)
    blank = jnp.zeros((MROWS, BLK), jnp.bfloat16)
    y_orders, z_orders = [spread(y, h) for h in range(2)], [spread(z, h) for h in range(2)]

    def unit(half, y_at, z_at):
        column = ((y_at * SIDE + z_at) * OWN + 2 * half) * BLK
        total = None
        for slot in range(MB):
            at = pl.ds(slot * MROWS, MROWS)
            one = rows[at, pl.ds(pl.multiple_of(column, 2 * BLK), BLK)]
            two = rows[at, pl.ds(pl.multiple_of(column + BLK, BLK), BLK)]
            left = jnp.concatenate([one, two], axis=0)
            right = jnp.concatenate(
                [jnp.concatenate([one, blank], axis=1), jnp.concatenate([blank, two], axis=1)],
                axis=0,
            )
            term = weights[slot] * lax.dot_general(
                left, right, (((0,), (0,)), ((), ())), preferred_element_type=jnp.float32
            )
            total = term if total is None else total + term
        first, second = total[:, :BLK], total[:, BLK:]
        square = jnp.where(row_at >= col_at, first, second)
        diagonal = jnp.sum(jnp.where(row_at == col_at, second, 0.0), axis=0, keepdims=True)
        return square, diagonal

    def put(place, words, marks):
        place[:CODED, :] = words
        for i, mark in enumerate(marks):
            place[CODED + i:CODED + i + 1, :] = mark

    def compute_give(chunk):
        for half in range(2):
            for i in range(2):
                square, diagonal = unit(half, y_orders[half][i], z_orders[half][chunk])
                words, marks = encode(square, diagonal, row_at, col_at)
                put(give.at[half, i, chunk], words, marks)

    def compute_keep(chunk):
        for half in range(2):
            for i, ref in enumerate((pass_on, keep)):
                square, diagonal = unit(half, y_orders[half][2 + i], z_orders[half][chunk])
                ref[half, chunk, :BLK, :] = square
                ref[half, chunk, BLK:, :] = jnp.broadcast_to(diagonal, (8, BLK))

    def remote(src, dst, send, recv, to):
        return pltpu.make_async_remote_copy(
            src_ref=src, dst_ref=dst, send_sem=send, recv_sem=recv,
            device_id=(to[0], to[1] * SIDE + to[2]), device_id_type=MESH,
        )

    y_first = [flip1(y), flip3(y)]
    y_second = [flip3(y), flip1(y)]
    z_first = [flip1(z), flip3(z)]
    z_second = [flip3(z), flip1(z)]
    to_s, to_y = final_target(s, y)
    halves, chunks = range(2), range(SIDE)

    step_y1 = [[[remote(give.at[h, i, c], got_y1.at[h, i, c], y1_send, y1_recv.at[h, i, c],
                        (s, y_first[h], z)) for c in chunks] for i in range(2)] for h in halves]
    step_y2 = [[remote(coded.at[h, c], got_y2.at[h, c], y2_send, y2_recv.at[h, c],
                       (s, y_second[h], z)) for c in chunks] for h in halves]
    step_z1 = [remote(keep.at[h, 0], got_z1.at[h], z1_send, z1_recv.at[h],
                      (s, y, z_first[h])) for h in halves]
    step_f = [[remote(keep.at[h, 1 + j], got_f.at[h, j], f_send, f_recv.at[h],
                      (to_s, to_y, to_z))
               for j, to_z in enumerate((z_first[h], z_second[h], z))] for h in halves]
    def start_y1(i, c):
        for h in halves:
            step_y1[h][i][c].start()

    def unpack(place):
        marks = [place[CODED + i:CODED + i + 1] for i in range(3)]
        return decode(place[:CODED], marks, row_at, col_at)

    def after_y1(c):
        for h in halves:
            step_y1[h][0][c].wait_recv()
            square, diagonal = unpack(got_y1.at[h, 0, c])
            words, marks = encode(
                pass_on[h, c, :BLK] + square, pass_on[h, c, BLK:BLK + 1] + diagonal,
                row_at, col_at,
            )
            put(coded.at[h, c], words, marks)
            step_y2[h][c].start()

    def finish(c):
        for h in halves:
            step_y1[h][1][c].wait_recv()
            square, diagonal = unpack(got_y1.at[h, 1, c])
            square, diagonal = keep[h, c, :BLK] + square, keep[h, c, BLK:BLK + 1] + diagonal
            step_y2[h][c].wait_recv()
            more, extra = unpack(got_y2.at[h, c])
            square, diagonal = square + more, diagonal + extra
            if c == 2:
                step_z1[h].wait_recv()
                square = square + got_z1[h, :BLK]
                diagonal = diagonal + got_z1[h, BLK:BLK + 1]
            keep[h, c, :BLK] = square
            keep[h, c, BLK:BLK + 1] = diagonal
            (step_z1[h] if c == 0 else step_f[h][c - 1]).start()

    fetched(0)
    compute_give(0)
    pl.semaphore_wait(barrier, len(greet))
    start_y1(0, 0)
    fetched(1)
    compute_give(1)
    start_y1(0, 1)
    start_y1(1, 0)
    compute_keep(0)
    compute_give(2)
    after_y1(0)
    start_y1(0, 2)
    start_y1(1, 1)
    compute_keep(1)
    after_y1(1)
    compute_give(3)
    start_y1(0, 3)
    compute_keep(2)
    finish(0)
    start_y1(1, 2)
    after_y1(2)
    compute_keep(3)
    start_y1(1, 3)
    finish(1)
    after_y1(3)
    finish(2)
    finish(3)
    weight_sum = jnp.float32(0.0)
    for m in range(MB):
        for other in range(REPLICAS):
            weight_sum = weight_sum + weight_table[m, other]
    shrink = 1.0 / (MROWS * jnp.full((8, BLK), weight_sum))[:1]
    here = (s, y_first[0], z)
    remote(give, got_y1, y1_send, z1_recv.at[0], here).wait_send()
    remote(coded, got_y2, y2_send, z1_recv.at[0], here).wait_send()
    remote(got_z1, got_z1, z1_send, z1_recv.at[0], here).wait_send()
    for h in halves:
        remote(got_f.at[h], got_f.at[h], f_send, f_recv.at[h], here).wait_recv()
        out[h] = (got_f[h, 0] + got_f[h, 1] + got_f[h, 2]) * shrink
    remote(got_f, got_f, f_send, f_recv.at[0], here).wait_send()


def reduce_blocks(sent_act, sent_grad, embedded, loss_grad, micro_weight, order):
    dma = pltpu.SemaphoreType.DMA
    block = (PACKED, BLK)
    message = (CODED + 8, BLK)
    hbm = pl.BlockSpec(memory_space=pltpu.HBM)
    return pl.pallas_call(
        reduce_kernel,
        out_shape=jax.ShapeDtypeStruct((2, PACKED, BLK), jnp.float32),
        in_specs=[hbm] * 6,
        out_specs=pl.BlockSpec(memory_space=pltpu.VMEM),
        scratch_shapes=[
            pltpu.VMEM((ROWS, 2 * D), jnp.bfloat16),
            pltpu.VMEM((2, 2, SIDE) + message, jnp.int32),
            pltpu.VMEM((2, SIDE) + block, jnp.float32),
            pltpu.VMEM((2, SIDE) + message, jnp.int32),
            pltpu.VMEM((2, SIDE) + block, jnp.float32),
            pltpu.VMEM((2, 2, SIDE) + message, jnp.int32),
            pltpu.VMEM((2, SIDE) + message, jnp.int32),
            pltpu.VMEM((2,) + block, jnp.float32),
            pltpu.VMEM((2, 3) + block, jnp.float32),
            pltpu.SMEM((MB, REPLICAS), jnp.float32),
            pltpu.SMEM((MB, SECTIONS), jnp.int32),
            dma((2,)), dma((2,)),
            dma, dma((2, 2, SIDE)), dma, dma((2, SIDE)), dma, dma((2,)), dma, dma((2,)),
        ],
        compiler_params=pltpu.CompilerParams(
            collective_id=0, has_side_effects=True, vmem_limit_bytes=VMEM_LIMIT
        ),
        name="gram_reduce",
    )(sent_act, sent_grad, embedded, loss_grad, micro_weight, order)


def split3(x):
    high = x.astype(jnp.bfloat16)
    rest = x - high.astype(jnp.float32)
    middle = rest.astype(jnp.bfloat16)
    low = (rest - middle.astype(jnp.float32)).astype(jnp.bfloat16)
    return high, middle, low


def dot(x, y):
    return lax.dot_general(x, y, (((1,), (0,)), ((), ())), preferred_element_type=jnp.float32)


def narrow(x):
    return x.astype(jnp.bfloat16)


def total(x):
    return jnp.sum(jnp.sum(x, axis=0, keepdims=True), axis=1, keepdims=True)


def dot_exact(x, y):
    h0, m0, l0 = split3(x)
    h1, m1, l1 = split3(y)
    left = jnp.concatenate([l0, h0, m0, m0, h0, h0], axis=1)
    right = jnp.concatenate([h1, l1, m1, h1, m1, h1], axis=0)
    return dot(left, right)


def sweep(work):
    sub = lax.broadcasted_iota(jnp.int32, (PANEL, BLK), 0)
    lane = lax.broadcasted_iota(jnp.int32, (PANEL, BLK), 1)
    col_at = lax.broadcasted_iota(jnp.int32, (BLK, BLK), 1)

    def spread_row(x, k):
        return jnp.broadcast_to(x[k:k + 1, :], (PANEL, BLK))

    for p in range(BLK // PANEL):
        start = p * PANEL
        inside = (lane >= start) & (lane < start + PANEL)
        panel_cols = (col_at >= start) & (col_at < start + PANEL)
        original = [work[m, start:start + PANEL, :] for m in range(OWN)]
        state = list(original)
        columns = [
            [jnp.broadcast_to(x[:, start + j:start + j + 1], (PANEL, BLK)) for j in range(PANEL)]
            for x in original
        ]
        for k in range(PANEL):
            for m in range(OWN):
                here = columns[m][k]
                inverse = 1.0 / spread_row(here, k)
                marked = jnp.where(lane == start + k, jnp.where(sub == k, 1.0, 0.0), state[m])
                pivot_row = spread_row(marked, k) * inverse
                state[m] = jnp.where(sub == k, pivot_row, marked - here * pivot_row)
                for j in range(k + 1, PANEL):
                    step = spread_row(columns[m][j], k) * inverse
                    columns[m][j] = jnp.where(sub == k, step, columns[m][j] - here * step)
        for m in range(OWN):
            swept = jnp.where(inside, -state[m], state[m])
            h0, m0, l0 = split3(original[m])
            h1, m1, l1 = split3(swept)
            left = jnp.concatenate([h0, h0, m0, m0, h0, l0], axis=0)
            right = jnp.concatenate([h1, m1, h1, m1, l1, h1], axis=0)
            update = lax.dot_general(
                left, right, (((0,), (0,)), ((), ())), preferred_element_type=jnp.float32
            )
            work[m] = jnp.where(panel_cols, 0.0, work[m]) - update
            work[m, start:start + PANEL, :] = swept


def invert_kernel(assignment, packed, old_hbm, out_hbm, work, old, out, mask, sems):
    r = lax.axis_index("dp")
    get_old = pltpu.make_async_copy(old_hbm, old, sems.at[0])
    get_mask = pltpu.make_async_copy(assignment, mask, sems.at[1])
    get_old.start()
    get_mask.start()
    row_at = lax.broadcasted_iota(jnp.int32, (BLK, BLK), 0)
    col_at = lax.broadcasted_iota(jnp.int32, (BLK, BLK), 1)
    on_diagonal = row_at == col_at
    identity = jnp.where(on_diagonal, 1.0, 0.0)
    for half in range(2):
        square = packed[half, :BLK, :]
        flipped = square.T
        one = jnp.where(row_at >= col_at, square, flipped)
        two = jnp.where(row_at < col_at, square, flipped)
        two = jnp.where(on_diagonal, packed[half, BLK:BLK + 1, :], two)
        work[2 * half] = one + damping * identity
        work[2 * half + 1] = two + damping * identity

    every = range(OWN)
    factors = [work[m] for m in every]
    spots = [jnp.where(on_diagonal, x, 0.0) for x in factors]
    along = [lax.rsqrt(jnp.sum(x, axis=0, keepdims=True)) for x in spots]
    down = [lax.rsqrt(jnp.sum(x, axis=1, keepdims=True)) for x in spots]
    unit = [factors[m] * along[m] * down[m] for m in every]
    gains = [BLK / total(x * x) for x in unit]
    power = [identity - gains[m] * unit[m] for m in every]
    series = [identity + x for x in power]
    power = [dot(narrow(x), narrow(x)) for x in power]
    for _ in range(ROUNDS):
        both = [
            dot(narrow(power[m]),
                jnp.concatenate([narrow(power[m]), narrow(series[m])], axis=1)) for m in every
        ]
        series = [series[m] + both[m][:, BLK:] for m in every]
        power = [x[:, :BLK] for x in both]
    series = [series[m] + dot(narrow(power[m]), narrow(series[m])) for m in every]
    guess = [gains[m] * series[m] for m in every]
    rest = [identity - dot_exact(unit[m], guess[m]) for m in every]
    square = [dot(narrow(x), narrow(x)) for x in rest]
    size = [total(x * x) for x in square]
    worst = jnp.maximum(jnp.maximum(size[0], size[1]), jnp.maximum(size[2], size[3]))
    square = [square[m] + dot(narrow(square[m]), narrow(rest[m])) for m in every]
    change = [rest[m] + square[m] for m in every]
    fresh = [guess[m] + dot_exact(guess[m], change[m]) for m in every]
    for m in every:
        out[0, m] = fresh[m] * along[m] * down[m]

    @pl.when(jnp.logical_not(worst[0, 0] <= LIMIT))
    def _():
        sweep(work)
        for m in every:
            out[0, m] = -work[m]

    get_old.wait()
    get_mask.wait()
    puts = []
    for m in every:
        refreshed = mask[0, r * OWN + m] < REPLICAS
        out[0, m] = jnp.where(refreshed, out[0, m], old[0, m])
        puts.append(pltpu.make_async_copy(out.at[0, m], out_hbm.at[0, m], sems.at[2 + m]))
        puts[m].start()
    for put in puts:
        put.wait()


def invert_blocks(assignment, packed, old_inverse):
    vmem, hbm = pl.BlockSpec(memory_space=pltpu.VMEM), pl.BlockSpec(memory_space=pltpu.HBM)
    return pl.pallas_call(
        invert_kernel,
        out_shape=jax.ShapeDtypeStruct(old_inverse.shape, jnp.float32),
        in_specs=[hbm, vmem, hbm],
        out_specs=hbm,
        scratch_shapes=[
            pltpu.VMEM((OWN, BLK, BLK), jnp.float32),
            pltpu.VMEM((1, OWN, BLK, BLK), jnp.float32),
            pltpu.VMEM((1, OWN, BLK, BLK), jnp.float32),
            pltpu.SMEM((1, NBLK), jnp.int32),
            pltpu.SemaphoreType.DMA((2 + OWN,)),
        ],
        compiler_params=pltpu.CompilerParams(vmem_limit_bytes=VMEM_LIMIT),
        name="invert",
    )(assignment, packed, old_inverse)


def shards(sent_act, sent_grad, embedded, loss_grad, micro_weight, order, assignment, old_inverse):
    packed = reduce_blocks(sent_act, sent_grad, embedded, loss_grad, micro_weight.T, order.T)
    return invert_blocks(assignment, packed, old_inverse)


def solution(mesh):
    in_specs = (
        P("section", "dp", None),
        P("section", "dp", None),
        P("dp", None),
        P("dp", None),
        P(),
        P(),
        P("section", None),
        P("section", "dp", None, None),
    )
    out_specs = P("section", "dp", None, None)
    return jax.shard_map(shards, mesh=mesh, in_specs=in_specs, out_specs=out_specs, check_vma=False)
```

```python
import jax
import jax.numpy as jnp
from jax import lax
from jax.experimental import pallas as pl
from jax.experimental.pallas import tpu as pltpu
from jax.sharding import PartitionSpec as P

D = 4096
BLK = 128
MB = 4
MROWS = 64
ROWS = MB * MROWS
NBLK = 64
OWN = 4
SIDE = 4
SECTIONS = 16
REPLICAS = 16
PACKED = BLK + 1
QUARTER = BLK // 4
CODED = 3 * QUARTER
BITS = 22.0
PANEL = 8
ROUNDS = 2
LIMIT = 1e-6
VMEM_LIMIT = 60 * 1024 * 1024
MESH = pl.DeviceIdType.MESH

damping = 0.1


def flip1(v):
    return v + 1 - 2 * (v % 2)


def flip2(v):
    return (v + 2) % 4


def flip3(v):
    return 3 - v


def spread(v, half):
    if half == 0:
        return flip2(v), flip1(v), flip3(v), v
    return flip2(v), flip3(v), flip1(v), v


def final_target(s, y):
    low, last, inner = 1 - y // 2, s // (SECTIONS - 1), (s + SECTIONS - 1) // SECTIONS
    to_s = s + low * (1 - last) - (1 - low) * inner
    to_y = y + 2 * low * last - 2 * (1 - low) * (1 - inner)
    return to_s, to_y


def final_source(s, y):
    low, last, inner = 1 - y // 2, s // (SECTIONS - 1), (s + SECTIONS - 1) // SECTIONS
    from_s = s - low * inner + (1 - low) * (1 - last)
    from_y = y + 2 * low * (1 - inner) - 2 * (1 - low) * last
    return from_s, from_y


def encode(square, diagonal, row_at, col_at):
    first = jnp.sum(jnp.where(row_at == col_at, square, 0.0), axis=0, keepdims=True)
    marks = []
    for entry in (first, diagonal):
        entry = jnp.maximum(entry, 1e-30)
        largest = jnp.max(entry, axis=1, keepdims=True)
        marks.append(jnp.ceil(0.5 * (jnp.log2(entry) + jnp.log2(largest))))
    gain = [jnp.exp2(BITS - mark) for mark in marks]
    values = (square * jnp.where(row_at >= col_at, gain[0], gain[1])).astype(jnp.int32)
    part = [values[i * QUARTER:(i + 1) * QUARTER] for i in range(4)]
    words = [(part[i] << 8) | ((part[3] >> (8 * i)) & 255) for i in range(3)]
    fine = (diagonal * (gain[1] * 256.0)).astype(jnp.int32)
    return (jnp.concatenate(words, axis=0),
            (marks[0].astype(jnp.int32), marks[1].astype(jnp.int32), fine))


def decode(words, marks, row_at, col_at):
    part = [words[i * QUARTER:(i + 1) * QUARTER] for i in range(3)]
    last = (part[0] & 255) | ((part[1] & 255) << 8) | ((part[2] & 255) << 16)
    values = jnp.concatenate([x >> 8 for x in part] + [(last << 8) >> 8], axis=0)
    step = [jnp.exp2(mark.astype(jnp.float32) - BITS) for mark in marks[:2]]
    square = values.astype(jnp.float32) * jnp.where(row_at >= col_at, step[0], step[1])
    return square, marks[2].astype(jnp.float32) * (step[1] * (1.0 / 256.0))


def reduce_kernel(
    sent_act, sent_grad, embedded, loss_grad, micro_weight, order, out,
    rows, give, pass_on, coded, keep, got_y1, got_y2, got_z1, got_f,
    weight_table, order_table, in_sem, table_sem,
    y1_send, y1_recv, y2_send, y2_recv, z1_send, z1_recv, f_send, f_recv,
):
    s = lax.axis_index("section")
    r = lax.axis_index("dp")
    y, z = r // SIDE, r % SIDE

    barrier = pltpu.get_barrier_semaphore()
    from_s, from_y = final_source(s, y)
    greet = [(s, flip1(y), z), (s, flip3(y), z), (s, y, flip1(z)), (s, y, flip3(z))]
    greet += [(from_s, from_y, z), (from_s, from_y, flip1(z)), (from_s, from_y, flip3(z))]
    for to_s, to_y, to_z in greet:
        pl.semaphore_signal(
            barrier, inc=1, device_id=(to_s, to_y * SIDE + to_z), device_id_type=MESH
        )

    tables = [
        pltpu.make_async_copy(micro_weight, weight_table, table_sem.at[0]),
        pltpu.make_async_copy(order, order_table, table_sem.at[1]),
    ]

    def fetch(src, to_y, place):
        first = (to_y * SIDE + flip2(z)) * OWN * BLK
        second = (to_y * SIDE + z // 2 * 2) * OWN * BLK
        third = (to_y * SIDE + z // 2 * -2 + 2 + (z + 1) % 2) * OWN * BLK
        column = (first, second, third)[place]
        size = (OWN, 2 * OWN, OWN)[place] * BLK
        wide = pl.ds(pl.multiple_of(column, size), size)
        narrow = pl.ds(pl.multiple_of(column - to_y // 2 * D, size), size)
        return pltpu.make_async_copy(
            src.at[:, narrow], rows.at[:, wide], in_sem.at[place]
        )

    for place in range(3):
        @pl.when(s < SECTIONS - 1)
        def _():
            for to_y in range(2):
                fetch(sent_act.at[0], to_y, place).start()

        @pl.when(s == SECTIONS - 1)
        def _():
            for to_y in range(2):
                fetch(loss_grad, to_y, place).start()

        @pl.when(s > 0)
        def _():
            for to_y in range(2, 4):
                fetch(sent_grad.at[0], to_y, place).start()

        @pl.when(s == 0)
        def _():
            for to_y in range(2, 4):
                fetch(embedded, to_y, place).start()

        if place == 0:
            for table in tables:
                table.start()

    def fetched(place):
        size = (4, 8, 4)[place] * OWN * BLK
        pltpu.make_async_copy(
            sent_act.at[0, :, pl.ds(0, size)], rows.at[:, pl.ds(0, size)], in_sem.at[place]
        ).wait()

    for table in tables:
        table.wait()
    weights = []
    for slot in range(MB):
        batch = order_table[slot, s]
        weight = jnp.float32(0.0)
        for m in range(MB):
            weight = weight + jnp.where(batch == m, weight_table[m, r], 0.0)
        weights.append(weight)

    row_at = lax.broadcasted_iota(jnp.int32, (BLK, BLK), 0)
    col_at = lax.broadcasted_iota(jnp.int32, (BLK, BLK), 1)
    blank = jnp.zeros((MROWS, BLK), jnp.bfloat16)
    y_orders, z_orders = [spread(y, h) for h in range(2)], [spread(z, h) for h in range(2)]

    def unit(half, y_at, z_at):
        column = ((y_at * SIDE + z_at) * OWN + 2 * half) * BLK
        total = None
        for slot in range(MB):
            at = pl.ds(slot * MROWS, MROWS)
            one = rows[at, pl.ds(pl.multiple_of(column, 2 * BLK), BLK)]
            two = rows[at, pl.ds(pl.multiple_of(column + BLK, BLK), BLK)]
            left = jnp.concatenate([one, two], axis=0)
            right = jnp.concatenate(
                [jnp.concatenate([one, blank], axis=1), jnp.concatenate([blank, two], axis=1)],
                axis=0,
            )
            term = weights[slot] * lax.dot_general(
                left, right, (((0,), (0,)), ((), ())), preferred_element_type=jnp.float32
            )
            total = term if total is None else total + term
        first, second = total[:, :BLK], total[:, BLK:]
        square = jnp.where(row_at >= col_at, first, second)
        diagonal = jnp.sum(jnp.where(row_at == col_at, second, 0.0), axis=0, keepdims=True)
        return square, diagonal

    def put(place, words, marks):
        place[:CODED, :] = words
        for i, mark in enumerate(marks):
            place[CODED + i:CODED + i + 1, :] = mark

    def compute_give(chunk):
        for half in range(2):
            for i in range(2):
                square, diagonal = unit(half, y_orders[half][i], z_orders[half][chunk])
                words, marks = encode(square, diagonal, row_at, col_at)
                put(give.at[half, i, chunk], words, marks)

    def compute_keep(chunk):
        for half in range(2):
            for i, ref in enumerate((pass_on, keep)):
                square, diagonal = unit(half, y_orders[half][2 + i], z_orders[half][chunk])
                ref[half, chunk, :BLK, :] = square
                ref[half, chunk, BLK:, :] = diagonal

    def remote(src, dst, send, recv, to):
        return pltpu.make_async_remote_copy(
            src_ref=src, dst_ref=dst, send_sem=send, recv_sem=recv,
            device_id=(to[0], to[1] * SIDE + to[2]), device_id_type=MESH,
        )

    y_first = [flip1(y), flip3(y)]
    y_second = [flip3(y), flip1(y)]
    z_first = [flip1(z), flip3(z)]
    z_second = [flip3(z), flip1(z)]
    to_s, to_y = final_target(s, y)
    halves, chunks = range(2), range(SIDE)

    step_y1 = [[[remote(give.at[h, i, c], got_y1.at[h, i, c], y1_send, y1_recv.at[h, i, c],
                        (s, y_first[h], z)) for c in chunks] for i in range(2)] for h in halves]
    step_y2 = [[remote(coded.at[h, c], got_y2.at[h, c], y2_send, y2_recv.at[h, c],
                       (s, y_second[h], z)) for c in chunks] for h in halves]
    step_z1 = [remote(keep.at[h, 0], got_z1.at[h], z1_send, z1_recv.at[h],
                      (s, y, z_first[h])) for h in halves]
    step_f = [[remote(keep.at[h, 1 + j], got_f.at[h, j], f_send, f_recv.at[h],
                      (to_s, to_y, to_z))
               for j, to_z in enumerate((z_first[h], z_second[h], z))] for h in halves]
    def start_y1(i, c):
        for h in halves:
            step_y1[h][i][c].start()

    def unpack(place):
        marks = [place[CODED + i:CODED + i + 1] for i in range(3)]
        return decode(place[:CODED], marks, row_at, col_at)

    def after_y1(c):
        for h in halves:
            step_y1[h][0][c].wait_recv()
            square, diagonal = unpack(got_y1.at[h, 0, c])
            words, marks = encode(
                pass_on[h, c, :BLK] + square, pass_on[h, c, BLK:BLK + 1] + diagonal,
                row_at, col_at,
            )
            put(coded.at[h, c], words, marks)
            step_y2[h][c].start()

    def finish(c):
        for h in halves:
            step_y1[h][1][c].wait_recv()
            square, diagonal = unpack(got_y1.at[h, 1, c])
            square, diagonal = keep[h, c, :BLK] + square, keep[h, c, BLK:BLK + 1] + diagonal
            step_y2[h][c].wait_recv()
            more, extra = unpack(got_y2.at[h, c])
            square, diagonal = square + more, diagonal + extra
            if c == 2:
                step_z1[h].wait_recv()
                square = square + got_z1[h, :BLK]
                diagonal = diagonal + got_z1[h, BLK:BLK + 1]
            keep[h, c, :BLK] = square
            keep[h, c, BLK:BLK + 1] = diagonal
            (step_z1[h] if c == 0 else step_f[h][c - 1]).start()

    fetched(0)
    compute_give(0)
    pl.semaphore_wait(barrier, len(greet))
    start_y1(0, 0)
    fetched(1)
    fetched(2)
    compute_give(1)
    start_y1(0, 1)
    start_y1(1, 0)
    compute_give(2)
    compute_keep(0)
    after_y1(0)
    start_y1(0, 2)
    start_y1(1, 1)
    compute_give(3)
    compute_keep(1)
    after_y1(1)
    start_y1(0, 3)
    start_y1(1, 2)
    finish(0)
    compute_keep(2)
    after_y1(2)
    start_y1(1, 3)
    compute_keep(3)
    finish(1)
    after_y1(3)
    finish(2)
    finish(3)
    weight_sum = jnp.float32(0.0)
    for m in range(MB):
        for other in range(REPLICAS):
            weight_sum = weight_sum + weight_table[m, other]
    shrink = 1.0 / (MROWS * jnp.full((8, BLK), weight_sum))[:1]
    here = (s, y_first[0], z)
    remote(give, got_y1, y1_send, z1_recv.at[0], here).wait_send()
    remote(coded, got_y2, y2_send, z1_recv.at[0], here).wait_send()
    remote(got_z1, got_z1, z1_send, z1_recv.at[0], here).wait_send()
    for h in halves:
        remote(got_f.at[h], got_f.at[h], f_send, f_recv.at[h], here).wait_recv()
        out[h] = (got_f[h, 0] + got_f[h, 1] + got_f[h, 2]) * shrink
    remote(got_f, got_f, f_send, f_recv.at[0], here).wait_send()


def reduce_blocks(sent_act, sent_grad, embedded, loss_grad, micro_weight, order):
    dma = pltpu.SemaphoreType.DMA
    block = (PACKED, BLK)
    message = (CODED + 3, BLK)
    hbm = pl.BlockSpec(memory_space=pltpu.HBM)
    return pl.pallas_call(
        reduce_kernel,
        out_shape=jax.ShapeDtypeStruct((2, PACKED, BLK), jnp.float32),
        in_specs=[hbm] * 6,
        out_specs=pl.BlockSpec(memory_space=pltpu.VMEM),
        scratch_shapes=[
            pltpu.VMEM((ROWS, 2 * D), jnp.bfloat16),
            pltpu.VMEM((2, 2, SIDE) + message, jnp.int32),
            pltpu.VMEM((2, SIDE) + block, jnp.float32),
            pltpu.VMEM((2, SIDE) + message, jnp.int32),
            pltpu.VMEM((2, SIDE) + block, jnp.float32),
            pltpu.VMEM((2, 2, SIDE) + message, jnp.int32),
            pltpu.VMEM((2, SIDE) + message, jnp.int32),
            pltpu.VMEM((2,) + block, jnp.float32),
            pltpu.VMEM((2, 3) + block, jnp.float32),
            pltpu.SMEM((MB, REPLICAS), jnp.float32),
            pltpu.SMEM((MB, SECTIONS), jnp.int32),
            dma((3,)), dma((2,)),
            dma, dma((2, 2, SIDE)), dma, dma((2, SIDE)), dma, dma((2,)), dma, dma((2,)),
        ],
        compiler_params=pltpu.CompilerParams(
            collective_id=0, has_side_effects=True, vmem_limit_bytes=VMEM_LIMIT
        ),
        name="gram_reduce",
    )(sent_act, sent_grad, embedded, loss_grad, micro_weight, order)


def split3(x):
    high = x.astype(jnp.bfloat16)
    rest = x - high.astype(jnp.float32)
    middle = rest.astype(jnp.bfloat16)
    low = (rest - middle.astype(jnp.float32)).astype(jnp.bfloat16)
    return high, middle, low


def dot(x, y):
    return lax.dot_general(x, y, (((1,), (0,)), ((), ())), preferred_element_type=jnp.float32)


def narrow(x):
    return x.astype(jnp.bfloat16)


def total(x):
    return jnp.sum(jnp.sum(x, axis=0, keepdims=True), axis=1, keepdims=True)


def dot_exact(x, y):
    h0, m0, l0 = split3(x)
    h1, m1, l1 = split3(y)
    left = jnp.concatenate([l0, h0, m0, m0, h0, h0], axis=1)
    right = jnp.concatenate([h1, l1, m1, h1, m1, h1], axis=0)
    return dot(left, right)


def sweep(work):
    sub = lax.broadcasted_iota(jnp.int32, (PANEL, BLK), 0)
    lane = lax.broadcasted_iota(jnp.int32, (PANEL, BLK), 1)
    col_at = lax.broadcasted_iota(jnp.int32, (BLK, BLK), 1)

    def spread_row(x, k):
        return jnp.broadcast_to(x[k:k + 1, :], (PANEL, BLK))

    for p in range(BLK // PANEL):
        start = p * PANEL
        inside = (lane >= start) & (lane < start + PANEL)
        panel_cols = (col_at >= start) & (col_at < start + PANEL)
        original = [work[m, start:start + PANEL, :] for m in range(OWN)]
        state = list(original)
        columns = [
            [jnp.broadcast_to(x[:, start + j:start + j + 1], (PANEL, BLK)) for j in range(PANEL)]
            for x in original
        ]
        for k in range(PANEL):
            for m in range(OWN):
                here = columns[m][k]
                inverse = 1.0 / spread_row(here, k)
                marked = jnp.where(lane == start + k, jnp.where(sub == k, 1.0, 0.0), state[m])
                pivot_row = spread_row(marked, k) * inverse
                state[m] = jnp.where(sub == k, pivot_row, marked - here * pivot_row)
                for j in range(k + 1, PANEL):
                    step = spread_row(columns[m][j], k) * inverse
                    columns[m][j] = jnp.where(sub == k, step, columns[m][j] - here * step)
        for m in range(OWN):
            swept = jnp.where(inside, -state[m], state[m])
            h0, m0, l0 = split3(original[m])
            h1, m1, l1 = split3(swept)
            left = jnp.concatenate([h0, h0, m0, m0, h0, l0], axis=0)
            right = jnp.concatenate([h1, m1, h1, m1, l1, h1], axis=0)
            update = lax.dot_general(
                left, right, (((0,), (0,)), ((), ())), preferred_element_type=jnp.float32
            )
            work[m] = jnp.where(panel_cols, 0.0, work[m]) - update
            work[m, start:start + PANEL, :] = swept


def invert_kernel(assignment, packed, old_hbm, out_hbm, work, old, out, mask, sems):
    r = lax.axis_index("dp")
    get_old = pltpu.make_async_copy(old_hbm, old, sems.at[0])
    get_mask = pltpu.make_async_copy(assignment, mask, sems.at[1])
    get_old.start()
    get_mask.start()
    row_at = lax.broadcasted_iota(jnp.int32, (BLK, BLK), 0)
    col_at = lax.broadcasted_iota(jnp.int32, (BLK, BLK), 1)
    on_diagonal = row_at == col_at
    identity = jnp.where(on_diagonal, 1.0, 0.0)
    for half in range(2):
        square = packed[half, :BLK, :]
        flipped = square.T
        one = jnp.where(row_at >= col_at, square, flipped)
        two = jnp.where(row_at < col_at, square, flipped)
        two = jnp.where(on_diagonal, packed[half, BLK:BLK + 1, :], two)
        work[2 * half] = one + damping * identity
        work[2 * half + 1] = two + damping * identity

    every = range(OWN)
    factors = [work[m] for m in every]
    spots = [jnp.where(on_diagonal, x, 0.0) for x in factors]
    along = [lax.rsqrt(jnp.sum(x, axis=0, keepdims=True)) for x in spots]
    down = [lax.rsqrt(jnp.sum(x, axis=1, keepdims=True)) for x in spots]
    unit = [factors[m] * along[m] * down[m] for m in every]
    gains = [BLK / total(x * x) for x in unit]
    power = [identity - gains[m] * unit[m] for m in every]
    series = [identity + x for x in power]
    power = [dot(narrow(x), narrow(x)) for x in power]
    for _ in range(ROUNDS):
        both = [
            dot(narrow(power[m]),
                jnp.concatenate([narrow(power[m]), narrow(series[m])], axis=1)) for m in every
        ]
        series = [series[m] + both[m][:, BLK:] for m in every]
        power = [x[:, :BLK] for x in both]
    series = [series[m] + dot(narrow(power[m]), narrow(series[m])) for m in every]
    guess = [gains[m] * series[m] for m in every]
    rest = [identity - dot_exact(unit[m], guess[m]) for m in every]
    square = [dot(narrow(x), narrow(x)) for x in rest]
    size = [total(x * x) for x in square]
    worst = jnp.maximum(jnp.maximum(size[0], size[1]), jnp.maximum(size[2], size[3]))
    square = [square[m] + dot(narrow(square[m]), narrow(rest[m])) for m in every]
    change = [rest[m] + square[m] for m in every]
    fresh = [guess[m] + dot_exact(guess[m], change[m]) for m in every]
    for m in every:
        out[0, m] = fresh[m] * along[m] * down[m]

    @pl.when(jnp.logical_not(worst[0, 0] <= LIMIT))
    def _():
        sweep(work)
        for m in every:
            out[0, m] = -work[m]

    get_old.wait()
    get_mask.wait()
    puts = []
    for m in every:
        refreshed = mask[0, r * OWN + m] < REPLICAS
        out[0, m] = jnp.where(refreshed, out[0, m], old[0, m])
        puts.append(pltpu.make_async_copy(out.at[0, m], out_hbm.at[0, m], sems.at[2 + m]))
        puts[m].start()
    for put in puts:
        put.wait()


def invert_blocks(assignment, packed, old_inverse):
    vmem, hbm = pl.BlockSpec(memory_space=pltpu.VMEM), pl.BlockSpec(memory_space=pltpu.HBM)
    return pl.pallas_call(
        invert_kernel,
        out_shape=jax.ShapeDtypeStruct(old_inverse.shape, jnp.float32),
        in_specs=[hbm, vmem, hbm],
        out_specs=hbm,
        scratch_shapes=[
            pltpu.VMEM((OWN, BLK, BLK), jnp.float32),
            pltpu.VMEM((1, OWN, BLK, BLK), jnp.float32),
            pltpu.VMEM((1, OWN, BLK, BLK), jnp.float32),
            pltpu.SMEM((1, NBLK), jnp.int32),
            pltpu.SemaphoreType.DMA((2 + OWN,)),
        ],
        compiler_params=pltpu.CompilerParams(vmem_limit_bytes=VMEM_LIMIT),
        name="invert",
    )(assignment, packed, old_inverse)


def shards(sent_act, sent_grad, embedded, loss_grad, micro_weight, order, assignment, old_inverse):
    packed = reduce_blocks(sent_act, sent_grad, embedded, loss_grad, micro_weight.T, order.T)
    return invert_blocks(assignment, packed, old_inverse)


def solution(mesh):
    in_specs = (
        P("section", "dp", None),
        P("section", "dp", None),
        P("dp", None),
        P("dp", None),
        P(),
        P(),
        P("section", None),
        P("section", "dp", None, None),
    )
    out_specs = P("section", "dp", None, None)
    return jax.shard_map(shards, mesh=mesh, in_specs=in_specs, out_specs=out_specs, check_vma=False)
```
